32 devices in a mesh: grp: 2 (over y), seq: 4 (over x, core), pos: 4 (over z).
Axes of the slice: x: 2, y: 2, z: 4, core: 2. Of those that a mesh axis runs over, the one named last changes fastest.
Arguments:
- couplings: bfloat16 [8, 3, 21, 21, 4096], P(('grp', 'pos')), parts along dimension 0, may hold values from -0.3984375 to 0.3984375
- fields: float32 [8, 21, 64], P(('grp', 'pos')), parts along dimension 0, may hold values from -6 to 300
- tokens: int32 [512, 512], P('grp', 'seq'), parts along dimension 0, may hold values from 0 to 20
- seq_weights: int32 [1024], P(('grp', 'seq')), parts along dimension 0, may hold values from 1 to 4
- block_cols: int32 [8, 3], P(('grp', 'pos')), parts along dimension 0, may hold values from 0 to 3, as said below
- block_count: int32 [8], P(('grp', 'pos')), parts along dimension 0, may hold values from 1 to 3, as said below
Outputs:
- grad_couplings: float32 [8, 3, 21, 21, 4096], P(('grp', 'pos'), None, None, None, 'seq'), parts along dimension 0
- grad_fields: float32 [8, 21, 64], P(('grp', 'pos')), parts along dimension 0
The draws below stay inside these ranges and needn't reach their ends.
There are 2 independent parts, one for each index of `grp`. The reference program is written for one: setup_inputs(seed, part) draws one part's arguments, and reference() takes and returns one part's arrays. A program takes and returns all parts, laid end to end along the dimension named above; each array names one. Nothing has to cross between parts.
Inputs may be any that keep to these rules, and one draw needn't show every extreme that they name: `block_cols`: each entry differs from the number of its own row block. Slots k >= block_count[r] of row block r are not live; some row block has exactly 3 live slots and some exactly 1.
All inputs are finite; a program needn't handle non-finite values.
Results may differ from the reference program's by a relative error of at most 0.0018.
Values may be sent and summed in bfloat16 or wider, within the bound.
No kernel may reach another device: no remote copies, remote signals or barrier semaphores. Data moves between devices by JAX's collectives and lax.ppermute only.
A program may use at most 192 MiB of HBM per device.

```python
import math
import jax
import jax.numpy as jnp
import numpy as np
from jax import lax

Q = 21
B = 64
KMAX = 3
NRB = 4
L = 256
SEQS = 512
BB = 4096


def draw_fields(key, part):
    keys = jax.random.split(key, 1)
    return jnp.clip(jax.random.normal(keys[0], (NRB, Q, B), jnp.float32), -6.0, 6.0)


def draw_block_cols(key, part):
    rows = jnp.arange(NRB, dtype=jnp.int32)[:, None]
    steps = jax.random.randint(jax.random.fold_in(key, 11), (NRB, KMAX), 0, NRB - 1)
    return (rows + 1 + steps) % NRB


def draw_block_count(key, part):
    keys = jax.random.split(jax.random.fold_in(key, 23), 3)
    counts = jax.random.randint(keys[0], (NRB,), 1, KMAX + 1)
    fullest = jax.random.randint(keys[1], (), 0, NRB)
    emptiest = (fullest + 1 + jax.random.randint(keys[2], (), 0, NRB - 1)) % NRB
    rows = jnp.arange(NRB, dtype=jnp.int32)
    counts = jnp.where(rows == fullest, KMAX, counts)
    return jnp.where(rows == emptiest, 1, counts).astype(jnp.int32)


def with_ends(result, key, low, largest):
    index_at = [jax.random.randint(jax.random.fold_in(key, axis), (), 0, length) for axis, length in enumerate(result.shape)]
    widest = result.shape.index(max(result.shape))
    neighbour = index_at[:widest] + [(index_at[widest] + 1) % result.shape[widest]] + index_at[widest + 1:]
    return result.at[tuple(index_at)].set(low).at[tuple(neighbour)].set(largest)


def steps_of(rng, shape, cuts, smallest, high):
    factor_of = 1.0
    for axis_at, shards_of in cuts:
        draws = jax.random.uniform(jax.random.fold_in(jax.random.fold_in(rng, 6), axis_at), (shards_of,), jnp.float32, smallest / len(cuts), high / len(cuts))
        factor_of = factor_of * jnp.repeat(jnp.exp(draws), shape[axis_at] // shards_of).reshape((-1,) + (1,) * (len(shape) - 1 - axis_at))
    return factor_of


def rank_bounds(number_of, lean):
    weights = [(1 << 20) // math.isqrt(standing ** lean) + 1 for standing in range(1, number_of + 1)]
    width = 1 + sum(weights) // (1 << 30)
    return np.cumsum(np.array([max(1, weight // width) for weight in weights]))


def ranked_ids(rng, extent, amount, lean):
    grid = rank_bounds(amount, lean)
    lot = jax.random.randint(jax.random.fold_in(rng, 1), extent, 0, int(grid[amount - 1]))
    standing = jnp.searchsorted(jnp.asarray(grid, jnp.int32), lot, side="right")
    return jax.random.permutation(jax.random.fold_in(rng, 2), amount)[standing].astype(jnp.int32)


def normal_values(own_key, extent, scale, reach, cuts=(), kind=jnp.bfloat16):
    array = jax.random.normal(own_key, extent, jnp.float32) * scale
    if len(cuts) > 0:
        array = steps_of(own_key, extent, cuts, -0.22, 0.18) * array
    return jnp.clip(array, min=-reach, max=reach).astype(kind)


def setup_inputs(seed: int = 0, part: int = 0) -> dict:
    streams_of = jax.random.split(jax.random.key(seed), 7)
    part_keys = jax.random.split(jax.random.fold_in(streams_of[6], part), 7)
    couplings = normal_values(part_keys[0], (NRB, KMAX, Q, Q, BB), 0.05, 0.3984375, ((0, 4),))
    fields = draw_fields(jax.random.fold_in(jax.random.fold_in(streams_of[6], part), 71), part)
    tokens = with_ends(ranked_ids(part_keys[2], (L, SEQS), Q, 2), jax.random.fold_in(part_keys[2], 3), 0, Q - 1).astype(jnp.int32)
    seq_weights = with_ends(jax.random.randint(part_keys[3], (SEQS,), 1, 5), jax.random.fold_in(part_keys[3], 1), 1, 4).astype(jnp.int32)
    block_cols = draw_block_cols(jax.random.fold_in(jax.random.fold_in(streams_of[6], part), 71), part)
    block_count = draw_block_count(jax.random.fold_in(jax.random.fold_in(streams_of[6], part), 71), part)
    return {"couplings": couplings, "fields": fields, "tokens": tokens, "seq_weights": seq_weights, "block_cols": block_cols, "block_count": block_count}


def add_block(total, index, block):
    current = lax.dynamic_index_in_dim(total, index, 0, keepdims=False)
    return lax.dynamic_update_index_in_dim(total, current + block, index, 0)


def reference(couplings, fields, tokens, seq_weights, block_cols, block_count):
    blocks_all, slot_count = block_cols.shape
    states = jnp.arange(Q, dtype=jnp.int32)
    onehot = (tokens.reshape(blocks_all, B, -1)[:, None, :, :] == states[None, :, None, None]).astype(jnp.float32)
    partials = jnp.zeros(onehot.shape, jnp.float32)
    for row_block in range(blocks_all):
        hot_row = onehot[row_block]
        for slot_index in range(slot_count):
            column = block_cols[row_block, slot_index].astype(jnp.int32)
            switch = (slot_index < block_count[row_block]).astype(jnp.float32)
            coupling = couplings[row_block, slot_index].astype(jnp.float32).reshape(Q, Q, B, B)
            hot_col = lax.dynamic_index_in_dim(onehot, column, 0, keepdims=False)
            own_term = jnp.einsum("abij,bjn->ain", coupling, hot_col, precision=lax.Precision.HIGHEST) * switch
            across = jnp.einsum("abij,ain->bjn", coupling, hot_row, precision=lax.Precision.HIGHEST) * switch
            partials = add_block(partials, row_block, own_term)
            partials = add_block(partials, column, across)
    logits = partials + fields[..., None]
    softmax_probs = jax.nn.softmax(logits, axis=1)
    seq_scale = seq_weights.astype(jnp.float32) / SEQS
    rounded = ((softmax_probs - onehot) * seq_scale).astype(jnp.bfloat16)
    residual = lax.optimization_barrier(rounded).astype(jnp.float32)
    grad_fields = jnp.sum(residual, axis=3)
    slot_grads = []
    for row_block in range(blocks_all):
        for slot_index in range(slot_count):
            column = block_cols[row_block, slot_index].astype(jnp.int32)
            switch = (slot_index < block_count[row_block]).astype(jnp.float32)
            hot_col = lax.dynamic_index_in_dim(onehot, column, 0, keepdims=False)
            res_col = lax.dynamic_index_in_dim(residual, column, 0, keepdims=False)
            first = jnp.einsum("ain,bjn->abij", residual[row_block], hot_col, precision=lax.Precision.HIGHEST)
            second = jnp.einsum("ain,bjn->abij", onehot[row_block], res_col, precision=lax.Precision.HIGHEST)
            slot_grads.append(((first + second) * switch).reshape(Q, Q, B * B))
    grad_couplings = jnp.stack(slot_grads).reshape(blocks_all, slot_count, Q, Q, B * B)
    return grad_couplings, grad_fields
```

```python
import functools

import jax
import jax.numpy as jnp
from jax import lax
from jax.experimental import pallas as pl
from jax.experimental.pallas import tpu as pltpu
from jax.sharding import PartitionSpec as P

Q = 21
B = 64
VMEM_BYTES = 56 * 1024 * 1024


def add_block(total, index, block):
    current = lax.dynamic_index_in_dim(total, index, 0, keepdims=False)
    return lax.dynamic_update_index_in_dim(total, current + block, index, 0)


def gated(is_live, compute):
    values = compute()
    switch = is_live.astype(jnp.float32)
    return tuple((value * switch for value in values))


def pair_matrix(coupling, states, width):
    square = coupling.reshape(states, states, width, width)
    return jnp.transpose(square, (0, 2, 1, 3)).reshape(states * width, states * width)


def pair_rows(res_row, hot_row, res_col, hot_col, row_count, col_count):
    seq_len = res_row.shape[-1]
    dims = (((1,), (1,)), ((), ()))
    first = lax.dot_general(
        res_row.reshape(Q * row_count, seq_len),
        hot_col.reshape(Q * col_count, seq_len),
        dims,
        preferred_element_type=jnp.float32,
    )
    second = lax.dot_general(
        hot_row.reshape(Q * row_count, seq_len),
        res_col.reshape(Q * col_count, seq_len),
        dims,
        preferred_element_type=jnp.float32,
    )
    table = (first + second).reshape(Q, row_count, Q, col_count)
    return jnp.transpose(table, (1, 3, 0, 2)).reshape(row_count * col_count, Q, Q)


def shards(couplings, fields, tokens, seq_weights, block_cols, block_count):
    rows_here, slot_count = block_cols.shape
    positions, seq_here = tokens.shape
    blocks_all = positions // B
    owner_index = lax.axis_index("pos")
    total_seqs = seq_here * lax.axis_size("seq")
    states = jnp.arange(Q, dtype=jnp.int32)
    onehot = (
        tokens.reshape(blocks_all, B, seq_here)[:, None, :, :] == states[None, :, None, None]
    ).astype(jnp.bfloat16)
    block_shape = (Q, B, seq_here)
    partials = jnp.zeros((blocks_all, Q, B, seq_here), jnp.float32)
    local_row = 0
    row_block = owner_index * rows_here + local_row
    hot_row = lax.dynamic_index_in_dim(onehot, row_block, 0, keepdims=False)
    for slot_index in range(slot_count):
        column = block_cols[local_row, slot_index]
        is_live = slot_index < block_count[local_row]
        matrix = pair_matrix(couplings[local_row, slot_index], Q, B)
        hot_col = lax.dynamic_index_in_dim(onehot, column, 0, keepdims=False)

        def contribute(matrix=matrix, hot_col=hot_col, hot_row=hot_row):
            own_term = jnp.dot(
                matrix, hot_col.reshape(Q * B, seq_here), preferred_element_type=jnp.float32
            )
            across = lax.dot_general(
                matrix,
                hot_row.reshape(Q * B, seq_here),
                (((0,), (0,)), ((), ())),
                preferred_element_type=jnp.float32,
            )
            return (own_term.reshape(block_shape), across.reshape(block_shape))

        own_term, across = gated(is_live, contribute)
        partials = add_block(partials, row_block, own_term)
        partials = add_block(partials, column, across)
    summed = lax.psum_scatter(
        partials.astype(jnp.bfloat16), "pos", scatter_dimension=0, tiled=True
    ).astype(jnp.float32)
    logits = summed + fields[..., None]
    softmax_probs = jax.nn.softmax(logits, axis=1)
    own_rows = lax.dynamic_slice_in_dim(onehot, owner_index * rows_here, rows_here, 0).astype(
        jnp.float32
    )
    seq_scale = seq_weights.astype(jnp.float32) / total_seqs
    residual = ((softmax_probs - own_rows) * seq_scale).astype(jnp.bfloat16)
    grad_fields = lax.psum(jnp.sum(residual.astype(jnp.float32), axis=3), "seq")
    residual_all = lax.all_gather(residual, "pos", axis=0, tiled=True)
    share_len = couplings.shape[-1] // lax.axis_size("seq")
    slot_grads = []
    local_row = 0
    row_block = owner_index * rows_here + local_row
    hot_row = lax.dynamic_index_in_dim(onehot, row_block, 0, keepdims=False)
    res_row = lax.dynamic_index_in_dim(residual_all, row_block, 0, keepdims=False)
    for slot_index in range(slot_count):
        column = block_cols[local_row, slot_index]
        is_live = slot_index < block_count[local_row]
        hot_col = lax.dynamic_index_in_dim(onehot, column, 0, keepdims=False)
        res_col = lax.dynamic_index_in_dim(residual_all, column, 0, keepdims=False)

        def slot_term(
            start,
            count,
            hot_row=hot_row,
            res_row=res_row,
            hot_col=hot_col,
            res_col=res_col,
            is_live=is_live,
        ):

            def compute():
                return (pair_rows(res_row, hot_row, res_col, hot_col, count // B, B),)

            (term,) = gated(is_live, compute)
            return term

        share = lax.psum_scatter(
            slot_term(jnp.int32(0), lax.axis_size("seq") * share_len),
            "seq",
            scatter_dimension=0,
            tiled=True,
        )
        slot_grads.append(jnp.transpose(share, (1, 2, 0)))
    grad_couplings = jnp.stack(slot_grads).reshape(rows_here, slot_count, Q, Q, share_len)
    return (grad_couplings, grad_fields)


def forward_kernel(cols, count, w, tok, own, near, mid, far, spread, table, hot_own, hot_col, acc_own, acc):
    slot = pl.program_id(0)
    seqs = tok.shape[1]
    pairs = B // 2
    lanes = 2 * B
    here = lax.axis_index("pos")
    lane = lax.broadcasted_iota(jnp.int32, (seqs, lanes), 1)

    @pl.when(slot == 0)
    def _():
        acc[...] = jnp.zeros_like(acc)
        acc_own[...] = jnp.zeros_like(acc_own)
        hot_col[...] = jnp.zeros_like(hot_col)
        table[Q * pairs :, :] = jnp.zeros((table.shape[0] - Q * pairs, table.shape[1]), table.dtype)
        for odd in range(2):
            ids = tok[pl.ds(here * B + odd, pairs, stride=2), :].astype(jnp.float32)
            ids = jnp.concatenate([ids] * 4, axis=0).T
            for tile in range(table.shape[0] // lanes):
                state = (4 * tile + lane // pairs).astype(jnp.float32)
                hot_own[odd * seqs : (odd + 1) * seqs, tile * lanes : (tile + 1) * lanes] = jnp.where(
                    ids == state, 1.0, 0.0
                ).astype(jnp.bfloat16)

    @pl.when(slot < count[0])
    def _():
        column = cols[0, slot]
        role = lax.bitwise_xor(column, here)

        def move(step, carry):
            for sub in range(3):
                a = step * 3 + sub
                for pair in range(pairs):
                    piece = w[0, a, :, pair * lanes : (pair + 1) * lanes].astype(jnp.float32)
                    spread[pl.ds(sub * Q * pairs + pair, Q, stride=pairs), :] = piece
                for b in range(Q):
                    at = sub * Q * pairs + b * pairs
                    table[pl.ds(pl.multiple_of(a * pairs, pairs), pairs), b * lanes : (b + 1) * lanes] = spread[
                        at : at + pairs, :
                    ].astype(jnp.bfloat16)
            return carry

        lax.fori_loop(0, Q // 3, move, 0)
        ids = tok[pl.ds(pl.multiple_of(column * B, B), B), :]
        for b in range(Q):
            hot = jnp.where(ids == b, 1.0, 0.0).astype(jnp.bfloat16)
            hot_col[b * lanes : b * lanes + B, :seqs] = hot
            hot_col[b * lanes + B : (b + 1) * lanes, seqs:] = hot
        acc_own[...] += jnp.dot(table[: Q * pairs, :], hot_col[...], preferred_element_type=jnp.float32)
        for b in range(0, Q, 2):
            width = 2 if b + 1 < Q else 1
            part = jnp.dot(
                hot_own[...],
                table[:, b * lanes : (b + width) * lanes],
                preferred_element_type=jnp.float32,
            )
            top0, low0 = part[:seqs, :lanes], part[seqs:, :lanes]
            if width == 2:
                top1, low1 = part[:seqs, lanes:], part[seqs:, lanes:]
            else:
                top1, low1 = top0, low0
            both = jnp.where(lane < B, top0, low1) + pltpu.roll(jnp.where(lane < B, top1, low0), B, 1)
            rows = slice(b * B, (b + width) * B)
            acc[role, rows, :] += both.T[: width * B, :]

    @pl.when(slot == pl.num_programs(0) - 1)
    def _():
        for odd in range(2):
            own[pl.ds(odd, Q * pairs, stride=2), :] = acc_own[:, odd * seqs : (odd + 1) * seqs]
        near[...] = acc[1].astype(jnp.bfloat16)
        mid[...] = acc[2].astype(jnp.bfloat16)
        far[...] = acc[3].astype(jnp.bfloat16)


def forward(couplings, tokens, block_cols, block_count):
    slots = couplings.shape[1]
    positions, seqs = tokens.shape
    rows, pairs, lanes = Q * B, B // 2, 2 * B
    depth = -(-Q * pairs // lanes) * lanes
    whole = pl.BlockSpec((rows, seqs), lambda k: (0, 0))
    smem = pl.BlockSpec(memory_space=pltpu.SMEM)
    return pl.pallas_call(
        forward_kernel,
        grid=(slots,),
        in_specs=[
            smem,
            smem,
            pl.BlockSpec((1, Q, Q, B * B), lambda k: (k, 0, 0, 0)),
            pl.BlockSpec((positions, seqs), lambda k: (0, 0)),
        ],
        out_specs=[whole] * 4,
        out_shape=[jax.ShapeDtypeStruct((rows, seqs), jnp.float32)]
        + [jax.ShapeDtypeStruct((rows, seqs), jnp.bfloat16)] * 3,
        scratch_shapes=[
            pltpu.VMEM((3 * Q * pairs, lanes), jnp.float32),
            pltpu.VMEM((depth, Q * lanes), jnp.bfloat16),
            pltpu.VMEM((2 * seqs, depth), jnp.bfloat16),
            pltpu.VMEM((Q * lanes, 2 * seqs), jnp.bfloat16),
            pltpu.VMEM((Q * pairs, 2 * seqs), jnp.float32),
            pltpu.VMEM((4, rows, seqs), jnp.float32),
        ],
        compiler_params=pltpu.CompilerParams(vmem_limit_bytes=VMEM_BYTES),
        cost_estimate=pl.CostEstimate(
            flops=2 * 4 * slots * rows * rows * seqs, bytes_accessed=2 * couplings.size, transcendentals=0
        ),
        name="forward",
    )(block_cols, block_count, couplings.reshape(slots, Q, Q, B * B), tokens)


def residual_kernel(total, own, first, second, fields, tok, weights, res):
    here = lax.axis_index("pos")
    step = 16
    scale = weights[...].astype(jnp.float32) / total
    field = fields[0].T
    for start in range(0, B, step):
        ids = tok[pl.ds(pl.multiple_of(here * B + start, step), step), :]
        logits = []
        for a in range(Q):
            rows = slice(a * B + start, a * B + start + step)
            terms = first[rows, :].astype(jnp.float32) + second[rows, :].astype(jnp.float32)
            logits.append(own[rows, :] + terms + field[start : start + step, a : a + 1])
        top = logits[0]
        for a in range(1, Q):
            top = jnp.maximum(top, logits[a])
        powers = [jnp.exp(value - top) for value in logits]
        norm = powers[0]
        for a in range(1, Q):
            norm = norm + powers[a]
        inverse = 1.0 / norm
        for a in range(Q):
            probs = powers[a] * inverse
            res[a * B + start : a * B + start + step, :] = (
                (probs - jnp.where(ids == a, 1.0, 0.0)) * scale
            ).astype(jnp.bfloat16)


def residuals(own, first, second, fields, tokens, seq_weights, total):
    rows, seqs = own.shape
    return pl.pallas_call(
        functools.partial(residual_kernel, total),
        out_shape=jax.ShapeDtypeStruct((rows, seqs), jnp.bfloat16),
        compiler_params=pltpu.CompilerParams(vmem_limit_bytes=VMEM_BYTES),
        cost_estimate=pl.CostEstimate(
            flops=20 * rows * seqs, bytes_accessed=10 * rows * seqs, transcendentals=rows * seqs
        ),
        name="residuals",
    )(own, first, second, fields, tokens, seq_weights.reshape(1, seqs))


def field_kernel(*refs):
    *parts, out = refs
    seqs = parts[0].shape[1]
    ones = jnp.ones((8, seqs), jnp.bfloat16)
    out[...] = sum(
        lax.dot_general(ones, part[...], (((1,), (1,)), ((), ())), preferred_element_type=jnp.float32)
        for part in parts
    )


def field_sums(parts):
    rows, seqs = parts[0].shape
    return pl.pallas_call(
        field_kernel,
        out_shape=jax.ShapeDtypeStruct((8, rows), jnp.float32),
        compiler_params=pltpu.CompilerParams(vmem_limit_bytes=VMEM_BYTES),
        cost_estimate=pl.CostEstimate(
            flops=16 * rows * seqs * len(parts), bytes_accessed=2 * rows * seqs * len(parts), transcendentals=0
        ),
        name="field_sums",
    )(*parts)


def gradient_kernel(role, shards_in, opening, *refs):
    cols, count = refs[:2]
    toks, mine, others = (refs[2 + g * shards_in : 2 + (g + 1) * shards_in] for g in range(3))
    out, left, right, spread, tiles, sems = refs[-6:]
    here, share = lax.axis_index("pos"), lax.axis_index("seq")
    slots = out.shape[0]
    seqs = toks[0].shape[1]
    depth = shards_in * seqs
    part = left.shape[0] // Q
    half = part // 2
    lanes = 2 * B
    dims = (((1,), (1,)), ((), ()))
    if opening:
        tiles[...] = jnp.zeros_like(tiles)
        for slot in range(slots):

            @pl.when(slot >= count[0])
            def _(slot=slot):
                copy = pltpu.make_async_copy(tiles, out.at[slot], sems.at[slot])
                copy.start()
                copy.wait()

    block = lax.bitwise_xor(here, role)
    wanted = [jnp.logical_and(slot < count[0], cols[0, slot] == block) for slot in range(slots)]
    needed = wanted[0]
    for flag in wanted[1:]:
        needed = jnp.logical_or(needed, flag)

    @pl.when(needed)
    def _():
        for n in range(shards_in):
            span = slice(n * seqs, (n + 1) * seqs)
            over = slice(depth + n * seqs, depth + (n + 1) * seqs)
            for a in range(Q):
                start = pl.multiple_of(a * B + share * part, part)
                spread[a * part : (a + 1) * part, :] = mine[n][pl.ds(start, part), :].astype(jnp.float32)
            start = here * B + share * part
            own_ids = jnp.concatenate(
                [toks[n][pl.ds(start + odd, half, stride=2), :] for odd in range(2)], axis=0
            )
            ids = toks[n][pl.ds(pl.multiple_of(block * B, B), B), :]
            for a in range(Q):
                piece = jnp.concatenate(
                    [spread[pl.ds(a * part + odd, half, stride=2), :] for odd in range(2)], axis=0
                )
                left[a * part : (a + 1) * part, span] = piece.astype(jnp.bfloat16)
                left[a * part : (a + 1) * part, over] = jnp.where(own_ids == a, 1.0, 0.0).astype(jnp.bfloat16)
                right[a * B : (a + 1) * B, span] = jnp.where(ids == a, 1.0, 0.0).astype(jnp.bfloat16)
            right[:, over] = others[n][...]
        lane = lax.broadcasted_iota(jnp.int32, (half, lanes), 1)
        for b in range(0, Q, 4):
            width = min(4, Q - b)
            rows = lax.dot_general(
                left[...], right[b * B : (b + width) * B, :], dims, preferred_element_type=jnp.float32
            )
            if width * B % lanes:
                rows = jnp.concatenate([rows, rows], axis=1)
            for a in range(Q):
                for pair in range(0, width, 2):
                    columns = slice(pair * B, pair * B + lanes)
                    even = rows[a * part : a * part + half, columns]
                    odd = rows[a * part + half : (a + 1) * part, columns]
                    at = (a * Q + b + pair) * half
                    tiles[at : at + half, :] = jnp.where(lane < B, even, pltpu.roll(odd, B, 1))
                    if pair + 1 < width:
                        tiles[at + half : at + 2 * half, :] = jnp.where(lane < B, pltpu.roll(even, B, 1), odd)
        for slot in range(slots):

            @pl.when(wanted[slot])
            def _(slot=slot):
                pltpu.make_async_copy(tiles, out.at[slot], sems.at[slot]).start()

        for slot in range(slots):

            @pl.when(wanted[slot])
            def _(slot=slot):
                pltpu.make_async_copy(tiles, out.at[slot], sems.at[slot]).wait()


def gradient(role, block_cols, block_count, toks, mine, others, done):
    slots = block_cols.shape[1]
    rows, seqs = mine[0].shape
    shards_in = len(toks)
    part = B // lax.axis_size("seq")
    smem = pl.BlockSpec(memory_space=pltpu.SMEM)
    vmem = pl.BlockSpec(memory_space=pltpu.VMEM)
    anywhere = pl.BlockSpec(memory_space=pl.ANY)
    operands = [block_cols, block_count, *toks, *mine, *others]
    specs = [smem, smem] + [vmem] * (3 * shards_in)
    aliases = {}
    if done is not None:
        aliases = {len(operands): 0}
        operands.append(done)
        specs.append(anywhere)
    height = Q * Q * part // 2
    return pl.pallas_call(
        functools.partial(gradient_kernel, role, shards_in, done is None),
        in_specs=specs,
        out_specs=anywhere,
        out_shape=jax.ShapeDtypeStruct((slots, height, 2 * B), jnp.float32),
        input_output_aliases=aliases,
        scratch_shapes=[
            pltpu.VMEM((Q * part, 2 * shards_in * seqs), jnp.bfloat16),
            pltpu.VMEM((rows, 2 * shards_in * seqs), jnp.bfloat16),
            pltpu.VMEM((Q * part, seqs), jnp.float32),
            pltpu.VMEM((height, 2 * B), jnp.float32),
            pltpu.SemaphoreType.DMA((slots,)),
        ],
        compiler_params=pltpu.CompilerParams(vmem_limit_bytes=VMEM_BYTES),
        cost_estimate=pl.CostEstimate(
            flops=4 * Q * part * rows * shards_in * seqs,
            bytes_accessed=4 * height * 2 * B + 4 * rows * seqs * shards_in,
            transcendentals=0,
        ),
        name="gradient",
    )(*operands)


def partner(bits, axis):
    return [(i, i ^ bits) for i in range(lax.axis_size(axis))]


def exchanged(value, bits, axis):
    return lax.ppermute(value, axis, partner(bits, axis))


def over_seq(value):
    along = exchanged(value, 2, "seq")
    return [value, along, exchanged(value, 1, "seq"), exchanged(along, 1, "seq")]


def shards_four(couplings, fields, tokens, seq_weights, block_cols, block_count):
    total_seqs = tokens.shape[1] * lax.axis_size("seq")
    toks = over_seq(tokens)
    own, near, mid, far = forward(couplings, tokens, block_cols, block_count)
    pair = far.astype(jnp.float32) + exchanged(mid, 1, "pos").astype(jnp.float32)
    first = exchanged(pair.astype(jnp.bfloat16), 3, "pos")
    second = exchanged(near, 1, "pos")
    res = residuals(own, first, second, fields, tokens, seq_weights, total_seqs)
    near_res = exchanged(res, 1, "pos")
    far_res = exchanged(res, 3, "pos")
    mid_res = exchanged(far_res, 1, "pos")
    mine = over_seq(res)
    grad = None
    for role, value in ((1, near_res), (3, far_res), (2, mid_res)):
        grad = gradient(role, block_cols, block_count, toks, mine, over_seq(value), grad)
    share_len = couplings.shape[-1] // lax.axis_size("seq")
    grad_fields = field_sums(mine)[:1].reshape(1, Q, B)
    return (grad.reshape(1, couplings.shape[1], Q, Q, share_len), grad_fields)


def solution(mesh):
    placed = (
        P(("grp", "pos"), None, None, None, None),
        P(("grp", "pos"), None, None),
        P("grp", "seq"),
        P(("grp", "seq")),
        P(("grp", "pos"), None),
        P(("grp", "pos")),
    )
    return jax.shard_map(
        shards_four if mesh.shape["pos"] == 4 and mesh.shape["seq"] == 4 else shards,
        mesh=mesh,
        in_specs=placed,
        out_specs=(P(("grp", "pos"), None, None, None, "seq"), P(("grp", "pos"), None, None)),
        check_vma=False,
    )
```

```python
import functools

import jax
import jax.numpy as jnp
from jax import lax
from jax.experimental import pallas as pl
from jax.experimental.pallas import tpu as pltpu
from jax.sharding import PartitionSpec as P

Q = 21
B = 64
VMEM_BYTES = 56 * 1024 * 1024


def add_block(total, index, block):
    current = lax.dynamic_index_in_dim(total, index, 0, keepdims=False)
    return lax.dynamic_update_index_in_dim(total, current + block, index, 0)


def gated(is_live, compute):
    values = compute()
    switch = is_live.astype(jnp.float32)
    return tuple((value * switch for value in values))


def pair_matrix(coupling, states, width):
    square = coupling.reshape(states, states, width, width)
    return jnp.transpose(square, (0, 2, 1, 3)).reshape(states * width, states * width)


def pair_rows(res_row, hot_row, res_col, hot_col, row_count, col_count):
    seq_len = res_row.shape[-1]
    dims = (((1,), (1,)), ((), ()))
    first = lax.dot_general(
        res_row.reshape(Q * row_count, seq_len),
        hot_col.reshape(Q * col_count, seq_len),
        dims,
        preferred_element_type=jnp.float32,
    )
    second = lax.dot_general(
        hot_row.reshape(Q * row_count, seq_len),
        res_col.reshape(Q * col_count, seq_len),
        dims,
        preferred_element_type=jnp.float32,
    )
    table = (first + second).reshape(Q, row_count, Q, col_count)
    return jnp.transpose(table, (1, 3, 0, 2)).reshape(row_count * col_count, Q, Q)


def shards(couplings, fields, tokens, seq_weights, block_cols, block_count):
    rows_here, slot_count = block_cols.shape
    positions, seq_here = tokens.shape
    blocks_all = positions // B
    owner_index = lax.axis_index("pos")
    total_seqs = seq_here * lax.axis_size("seq")
    states = jnp.arange(Q, dtype=jnp.int32)
    onehot = (
        tokens.reshape(blocks_all, B, seq_here)[:, None, :, :] == states[None, :, None, None]
    ).astype(jnp.bfloat16)
    block_shape = (Q, B, seq_here)
    partials = jnp.zeros((blocks_all, Q, B, seq_here), jnp.float32)
    local_row = 0
    row_block = owner_index * rows_here + local_row
    hot_row = lax.dynamic_index_in_dim(onehot, row_block, 0, keepdims=False)
    for slot_index in range(slot_count):
        column = block_cols[local_row, slot_index]
        is_live = slot_index < block_count[local_row]
        matrix = pair_matrix(couplings[local_row, slot_index], Q, B)
        hot_col = lax.dynamic_index_in_dim(onehot, column, 0, keepdims=False)

        def contribute(matrix=matrix, hot_col=hot_col, hot_row=hot_row):
            own_term = jnp.dot(
                matrix, hot_col.reshape(Q * B, seq_here), preferred_element_type=jnp.float32
            )
            across = lax.dot_general(
                matrix,
                hot_row.reshape(Q * B, seq_here),
                (((0,), (0,)), ((), ())),
                preferred_element_type=jnp.float32,
            )
            return (own_term.reshape(block_shape), across.reshape(block_shape))

        own_term, across = gated(is_live, contribute)
        partials = add_block(partials, row_block, own_term)
        partials = add_block(partials, column, across)
    summed = lax.psum_scatter(
        partials.astype(jnp.bfloat16), "pos", scatter_dimension=0, tiled=True
    ).astype(jnp.float32)
    logits = summed + fields[..., None]
    softmax_probs = jax.nn.softmax(logits, axis=1)
    own_rows = lax.dynamic_slice_in_dim(onehot, owner_index * rows_here, rows_here, 0).astype(
        jnp.float32
    )
    seq_scale = seq_weights.astype(jnp.float32) / total_seqs
    residual = ((softmax_probs - own_rows) * seq_scale).astype(jnp.bfloat16)
    grad_fields = lax.psum(jnp.sum(residual.astype(jnp.float32), axis=3), "seq")
    residual_all = lax.all_gather(residual, "pos", axis=0, tiled=True)
    share_len = couplings.shape[-1] // lax.axis_size("seq")
    slot_grads = []
    local_row = 0
    row_block = owner_index * rows_here + local_row
    hot_row = lax.dynamic_index_in_dim(onehot, row_block, 0, keepdims=False)
    res_row = lax.dynamic_index_in_dim(residual_all, row_block, 0, keepdims=False)
    for slot_index in range(slot_count):
        column = block_cols[local_row, slot_index]
        is_live = slot_index < block_count[local_row]
        hot_col = lax.dynamic_index_in_dim(onehot, column, 0, keepdims=False)
        res_col = lax.dynamic_index_in_dim(residual_all, column, 0, keepdims=False)

        def slot_term(
            start,
            count,
            hot_row=hot_row,
            res_row=res_row,
            hot_col=hot_col,
            res_col=res_col,
            is_live=is_live,
        ):

            def compute():
                return (pair_rows(res_row, hot_row, res_col, hot_col, count // B, B),)

            (term,) = gated(is_live, compute)
            return term

        share = lax.psum_scatter(
            slot_term(jnp.int32(0), lax.axis_size("seq") * share_len),
            "seq",
            scatter_dimension=0,
            tiled=True,
        )
        slot_grads.append(jnp.transpose(share, (1, 2, 0)))
    grad_couplings = jnp.stack(slot_grads).reshape(rows_here, slot_count, Q, Q, share_len)
    return (grad_couplings, grad_fields)


def relay(w, table):
    pairs, lanes = B // 2, 2 * B

    def move(step, carry):
        for sub in range(3):
            a = step * 3 + sub
            blocks = w[0, a].reshape(Q, pairs, lanes)
            for b in range(Q):
                table[pl.ds(pl.multiple_of(a * pairs, pairs), pairs), b * lanes : (b + 1) * lanes] = blocks[b]
        return carry

    lax.fori_loop(0, Q // 3, move, 0)


def own_kernel(cols, count, w, tok, own, table, hot_col, acc_own):
    slot = pl.program_id(0)
    seqs = tok.shape[1]
    pairs, lanes = B // 2, 2 * B

    @pl.when(slot == 0)
    def _():
        acc_own[...] = jnp.zeros_like(acc_own)
        hot_col[...] = jnp.zeros_like(hot_col)

    @pl.when(slot < count[0])
    def _():
        relay(w, table)
        ids = tok[pl.ds(pl.multiple_of(cols[0, slot] * B, B), B), :]
        for b in range(Q):
            hot = jnp.where(ids == b, 1.0, 0.0).astype(jnp.bfloat16)
            hot_col[b * lanes : b * lanes + B, :seqs] = hot
            hot_col[b * lanes + B : (b + 1) * lanes, seqs:] = hot
        acc_own[...] += jnp.dot(table[...], hot_col[...], preferred_element_type=jnp.float32)

    @pl.when(slot == pl.num_programs(0) - 1)
    def _():
        for odd in range(2):
            own[pl.ds(odd, Q * pairs, stride=2), :] = acc_own[:, odd * seqs : (odd + 1) * seqs]


def across_kernel(cols, count, w, tok, near, mid, far, table, hot_own, acc):
    slot = pl.program_id(0)
    seqs = tok.shape[1]
    pairs = B // 2
    lanes = 2 * B
    here = lax.axis_index("pos")
    lane = lax.broadcasted_iota(jnp.int32, (seqs, lanes), 1)

    @pl.when(slot == 0)
    def _():
        acc[...] = jnp.zeros_like(acc)
        table[Q * pairs :, :] = jnp.zeros((table.shape[0] - Q * pairs, table.shape[1]), table.dtype)
        for odd in range(2):
            ids = tok[pl.ds(here * B + odd, pairs, stride=2), :].astype(jnp.float32)
            ids = jnp.concatenate([ids] * 4, axis=0).T
            for tile in range(table.shape[0] // lanes):
                state = (4 * tile + lane // pairs).astype(jnp.float32)
                hot_own[odd * seqs : (odd + 1) * seqs, tile * lanes : (tile + 1) * lanes] = jnp.where(
                    ids == state, 1.0, 0.0
                ).astype(jnp.bfloat16)

    @pl.when(slot < count[0])
    def _():
        role = lax.bitwise_xor(cols[0, slot], here)
        relay(w, table)
        for b in range(0, Q, 2):
            width = 2 if b + 1 < Q else 1
            part = jnp.dot(
                hot_own[...],
                table[:, b * lanes : (b + width) * lanes],
                preferred_element_type=jnp.float32,
            )
            top0, low0 = part[:seqs, :lanes], part[seqs:, :lanes]
            if width == 2:
                top1, low1 = part[:seqs, lanes:], part[seqs:, lanes:]
            else:
                top1, low1 = top0, low0
            both = jnp.where(lane < B, top0, low1) + pltpu.roll(jnp.where(lane < B, top1, low0), B, 1)
            rows = slice(b * B, (b + width) * B)
            acc[role, rows, :] += both.T[: width * B, :]

    @pl.when(slot == pl.num_programs(0) - 1)
    def _():
        near[...] = acc[1].astype(jnp.bfloat16)
        mid[...] = acc[2].astype(jnp.bfloat16)
        far[...] = acc[3].astype(jnp.bfloat16)


def forward_call(kernel, name, outs, scratch, couplings, tokens, block_cols, block_count):
    slots = couplings.shape[1]
    positions, seqs = tokens.shape
    rows = Q * B
    smem = pl.BlockSpec(memory_space=pltpu.SMEM)
    return pl.pallas_call(
        kernel,
        grid=(slots,),
        in_specs=[
            smem,
            smem,
            pl.BlockSpec((1, Q, Q, B * B), lambda k: (k, 0, 0, 0)),
            pl.BlockSpec((positions, seqs), lambda k: (0, 0)),
        ],
        out_specs=[pl.BlockSpec((rows, seqs), lambda k: (0, 0))] * len(outs),
        out_shape=[jax.ShapeDtypeStruct((rows, seqs), dtype) for dtype in outs],
        scratch_shapes=scratch,
        compiler_params=pltpu.CompilerParams(vmem_limit_bytes=VMEM_BYTES),
        cost_estimate=pl.CostEstimate(
            flops=2 * 4 * slots * rows * rows * seqs, bytes_accessed=2 * couplings.size, transcendentals=0
        ),
        name=name,
    )(block_cols, block_count, couplings.reshape(slots, Q, Q, B * B), tokens)


def across_terms(couplings, tokens, block_cols, block_count):
    seqs, pairs, lanes = tokens.shape[1], B // 2, 2 * B
    depth = -(-Q * pairs // lanes) * lanes
    scratch = [
        pltpu.VMEM((depth, Q * lanes), jnp.bfloat16),
        pltpu.VMEM((2 * seqs, depth), jnp.bfloat16),
        pltpu.VMEM((4, Q * B, seqs), jnp.float32),
    ]
    return forward_call(
        across_kernel, "across", [jnp.bfloat16] * 3, scratch, couplings, tokens, block_cols, block_count
    )


def own_terms(couplings, tokens, block_cols, block_count):
    seqs, pairs, lanes = tokens.shape[1], B // 2, 2 * B
    scratch = [
        pltpu.VMEM((Q * pairs, Q * lanes), jnp.bfloat16),
        pltpu.VMEM((Q * lanes, 2 * seqs), jnp.bfloat16),
        pltpu.VMEM((Q * pairs, 2 * seqs), jnp.float32),
    ]
    (own,) = forward_call(
        own_kernel, "own", [jnp.float32], scratch, couplings, tokens, block_cols, block_count
    )
    return own


def residual_kernel(total, own, first, second, fields, tok, weights, res):
    here = lax.axis_index("pos")
    step = 16
    scale = weights[...].astype(jnp.float32) / total
    field = fields[0].T
    for start in range(0, B, step):
        ids = tok[pl.ds(pl.multiple_of(here * B + start, step), step), :]
        logits = []
        for a in range(Q):
            rows = slice(a * B + start, a * B + start + step)
            terms = first[rows, :].astype(jnp.float32) + second[rows, :].astype(jnp.float32)
            logits.append(own[rows, :] + terms + field[start : start + step, a : a + 1])
        top = logits[0]
        for a in range(1, Q):
            top = jnp.maximum(top, logits[a])
        powers = [jnp.exp(value - top) for value in logits]
        norm = powers[0]
        for a in range(1, Q):
            norm = norm + powers[a]
        inverse = 1.0 / norm
        for a in range(Q):
            probs = powers[a] * inverse
            res[a * B + start : a * B + start + step, :] = (
                (probs - jnp.where(ids == a, 1.0, 0.0)) * scale
            ).astype(jnp.bfloat16)


def residuals(own, first, second, fields, tokens, seq_weights, total):
    rows, seqs = own.shape
    return pl.pallas_call(
        functools.partial(residual_kernel, total),
        out_shape=jax.ShapeDtypeStruct((rows, seqs), jnp.bfloat16),
        compiler_params=pltpu.CompilerParams(vmem_limit_bytes=VMEM_BYTES),
        cost_estimate=pl.CostEstimate(
            flops=20 * rows * seqs, bytes_accessed=10 * rows * seqs, transcendentals=rows * seqs
        ),
        name="residuals",
    )(own, first, second, fields, tokens, seq_weights.reshape(1, seqs))


def prepare_kernel(shards_in, *refs):
    toks, mine = refs[:shards_in], refs[shards_in : 2 * shards_in]
    left, sums, spread = refs[2 * shards_in :]
    here, share = lax.axis_index("pos"), lax.axis_index("seq")
    seqs = toks[0].shape[1]
    depth = shards_in * seqs
    part = left.shape[0] // Q
    half = part // 2
    ones = jnp.ones((8, seqs), jnp.bfloat16)
    sums[...] = sum(
        lax.dot_general(ones, piece[...], (((1,), (1,)), ((), ())), preferred_element_type=jnp.float32)
        for piece in mine
    )
    for n in range(shards_in):
        span = slice(n * seqs, (n + 1) * seqs)
        over = slice(depth + n * seqs, depth + (n + 1) * seqs)
        for a in range(Q):
            start = pl.multiple_of(a * B + share * part, part)
            spread[a * part : (a + 1) * part, :] = mine[n][pl.ds(start, part), :].astype(jnp.float32)
        start = here * B + share * part
        ids = jnp.concatenate([toks[n][pl.ds(start + odd, half, stride=2), :] for odd in range(2)], axis=0)
        for a in range(Q):
            piece = jnp.concatenate(
                [spread[pl.ds(a * part + odd, half, stride=2), :] for odd in range(2)], axis=0
            )
            left[a * part : (a + 1) * part, span] = piece.astype(jnp.bfloat16)
            left[a * part : (a + 1) * part, over] = jnp.where(ids == a, 1.0, 0.0).astype(jnp.bfloat16)


def prepare(toks, mine):
    rows, seqs = mine[0].shape
    shards_in = len(toks)
    part = B // lax.axis_size("seq")
    return pl.pallas_call(
        functools.partial(prepare_kernel, shards_in),
        out_shape=[
            jax.ShapeDtypeStruct((Q * part, 2 * shards_in * seqs), jnp.bfloat16),
            jax.ShapeDtypeStruct((8, rows), jnp.float32),
        ],
        scratch_shapes=[pltpu.VMEM((Q * part, seqs), jnp.float32)],
        compiler_params=pltpu.CompilerParams(vmem_limit_bytes=VMEM_BYTES),
        cost_estimate=pl.CostEstimate(
            flops=16 * rows * seqs * shards_in, bytes_accessed=4 * rows * seqs * shards_in, transcendentals=0
        ),
        name="prepare",
    )(*toks, *mine)


def gradient_kernel(role, shards_in, opening, cols, count, left, *refs):
    toks, others = refs[:shards_in], refs[shards_in : 2 * shards_in]
    out, right, tiles, sems, arrived = refs[-5:]
    here = lax.axis_index("pos")
    slots = out.shape[0]
    seqs = toks[0].shape[1]
    depth = shards_in * seqs
    part = left.shape[0] // Q
    half = part // 2
    lanes = 2 * B
    dims = (((1,), (1,)), ((), ()))
    if opening:
        tiles[...] = jnp.zeros_like(tiles)
        for slot in range(slots):

            @pl.when(slot >= count[0])
            def _(slot=slot):
                copy = pltpu.make_async_copy(tiles, out.at[slot], sems.at[slot])
                copy.start()
                copy.wait()

    block = lax.bitwise_xor(here, role)
    wanted = [jnp.logical_and(slot < count[0], cols[0, slot] == block) for slot in range(slots)]
    needed = wanted[0]
    for flag in wanted[1:]:
        needed = jnp.logical_or(needed, flag)

    @pl.when(needed)
    def _():
        fetches = [
            pltpu.make_async_copy(
                others[n], right.at[:, pl.ds(depth + n * seqs, seqs)], arrived.at[n]
            )
            for n in range(shards_in)
        ]
        for fetch in fetches:
            fetch.start()
        for n in range(shards_in):
            span = slice(n * seqs, (n + 1) * seqs)
            ids = toks[n][pl.ds(pl.multiple_of(block * B, B), B), :]
            for b in range(Q):
                right[b * B : (b + 1) * B, span] = jnp.where(ids == b, 1.0, 0.0).astype(jnp.bfloat16)
        for fetch in fetches:
            fetch.wait()
        lane = lax.broadcasted_iota(jnp.int32, (half, lanes), 1)
        for b in range(0, Q, 4):
            width = min(4, Q - b)
            rows = lax.dot_general(
                left[...], right[b * B : (b + width) * B, :], dims, preferred_element_type=jnp.float32
            )
            if width * B % lanes:
                rows = jnp.concatenate([rows, rows], axis=1)
            for a in range(Q):
                for pair in range(0, width, 2):
                    columns = slice(pair * B, pair * B + lanes)
                    even = rows[a * part : a * part + half, columns]
                    odd = rows[a * part + half : (a + 1) * part, columns]
                    at = (a * Q + b + pair) * half
                    tiles[at : at + half, :] = jnp.where(lane < B, even, pltpu.roll(odd, B, 1))
                    if pair + 1 < width:
                        tiles[at + half : at + 2 * half, :] = jnp.where(lane < B, pltpu.roll(even, B, 1), odd)
        for slot in range(slots):

            @pl.when(wanted[slot])
            def _(slot=slot):
                pltpu.make_async_copy(tiles, out.at[slot], sems.at[slot]).start()

        for slot in range(slots):

            @pl.when(wanted[slot])
            def _(slot=slot):
                pltpu.make_async_copy(tiles, out.at[slot], sems.at[slot]).wait()


def gradient(role, block_cols, block_count, left, toks, others, done):
    slots = block_cols.shape[1]
    rows, seqs = others[0].shape
    shards_in = len(toks)
    part = B // lax.axis_size("seq")
    smem = pl.BlockSpec(memory_space=pltpu.SMEM)
    vmem = pl.BlockSpec(memory_space=pltpu.VMEM)
    anywhere = pl.BlockSpec(memory_space=pl.ANY)
    operands = [block_cols, block_count, left, *toks, *others]
    specs = [smem, smem, vmem] + [vmem] * shards_in + [anywhere] * shards_in
    aliases = {}
    if done is not None:
        aliases = {len(operands): 0}
        operands.append(done)
        specs.append(anywhere)
    height = Q * Q * part // 2
    return pl.pallas_call(
        functools.partial(gradient_kernel, role, shards_in, done is None),
        in_specs=specs,
        out_specs=anywhere,
        out_shape=jax.ShapeDtypeStruct((slots, height, 2 * B), jnp.float32),
        input_output_aliases=aliases,
        scratch_shapes=[
            pltpu.VMEM((rows, 2 * shards_in * seqs), jnp.bfloat16),
            pltpu.VMEM((height, 2 * B), jnp.float32),
            pltpu.SemaphoreType.DMA((slots,)),
            pltpu.SemaphoreType.DMA((shards_in,)),
        ],
        compiler_params=pltpu.CompilerParams(vmem_limit_bytes=VMEM_BYTES),
        cost_estimate=pl.CostEstimate(
            flops=4 * Q * part * rows * shards_in * seqs,
            bytes_accessed=4 * height * 2 * B + 4 * rows * seqs * shards_in,
            transcendentals=0,
        ),
        name="gradient",
    )(*operands)


def partner(bits, axis):
    return [(i, i ^ bits) for i in range(lax.axis_size(axis))]


def exchanged(value, bits, axis):
    return lax.ppermute(value, axis, partner(bits, axis))


def over_seq(value):
    along = exchanged(value, 2, "seq")
    return [value, along, exchanged(value, 1, "seq"), exchanged(along, 1, "seq")]


def shards_four(couplings, fields, tokens, seq_weights, block_cols, block_count):
    total_seqs = tokens.shape[1] * lax.axis_size("seq")
    toks = over_seq(tokens)
    near, mid, far = across_terms(couplings, tokens, block_cols, block_count)
    near, mid, far, *toks = lax.optimization_barrier((near, mid, far, *toks))
    pair = far.astype(jnp.float32) + exchanged(mid, 1, "pos").astype(jnp.float32)
    second = exchanged(near, 1, "pos")
    first = exchanged(pair.astype(jnp.bfloat16), 3, "pos")
    own = own_terms(couplings, tokens, block_cols, block_count)
    res = residuals(own, first, second, fields, tokens, seq_weights, total_seqs)
    near_res = exchanged(res, 1, "pos")
    far_res = exchanged(res, 3, "pos")
    mid_res = exchanged(far_res, 1, "pos")
    left, sums = prepare(toks, over_seq(res))
    grad = gradient(1, block_cols, block_count, left, toks, over_seq(near_res), None)
    mid_along = exchanged(mid_res, 2, "seq")
    grad, mid_along = lax.optimization_barrier((grad, mid_along))
    grad = gradient(3, block_cols, block_count, left, toks, over_seq(far_res), grad)
    mids = [mid_res, mid_along, exchanged(mid_res, 1, "seq"), exchanged(mid_along, 1, "seq")]
    grad = gradient(2, block_cols, block_count, left, toks, mids, grad)
    share_len = couplings.shape[-1] // lax.axis_size("seq")
    return (grad.reshape(1, couplings.shape[1], Q, Q, share_len), sums[:1].reshape(1, Q, B))


def solution(mesh):
    placed = (
        P(("grp", "pos"), None, None, None, None),
        P(("grp", "pos"), None, None),
        P("grp", "seq"),
        P(("grp", "seq")),
        P(("grp", "pos"), None),
        P(("grp", "pos")),
    )
    return jax.shard_map(
        shards_four if mesh.shape["pos"] == 4 and mesh.shape["seq"] == 4 else shards,
        mesh=mesh,
        in_specs=placed,
        out_specs=(P(("grp", "pos"), None, None, None, "seq"), P(("grp", "pos"), None, None)),
        check_vma=False,
    )
```

```python
import functools

import jax
import jax.numpy as jnp
from jax import lax
from jax.experimental import pallas as pl
from jax.experimental.pallas import tpu as pltpu
from jax.sharding import PartitionSpec as P

Q = 21
B = 64
VMEM_BYTES = 56 * 1024 * 1024


def add_block(total, index, block):
    current = lax.dynamic_index_in_dim(total, index, 0, keepdims=False)
    return lax.dynamic_update_index_in_dim(total, current + block, index, 0)


def gated(is_live, compute):
    values = compute()
    switch = is_live.astype(jnp.float32)
    return tuple((value * switch for value in values))


def pair_matrix(coupling, states, width):
    square = coupling.reshape(states, states, width, width)
    return jnp.transpose(square, (0, 2, 1, 3)).reshape(states * width, states * width)


def pair_rows(res_row, hot_row, res_col, hot_col, row_count, col_count):
    seq_len = res_row.shape[-1]
    dims = (((1,), (1,)), ((), ()))
    first = lax.dot_general(
        res_row.reshape(Q * row_count, seq_len),
        hot_col.reshape(Q * col_count, seq_len),
        dims,
        preferred_element_type=jnp.float32,
    )
    second = lax.dot_general(
        hot_row.reshape(Q * row_count, seq_len),
        res_col.reshape(Q * col_count, seq_len),
        dims,
        preferred_element_type=jnp.float32,
    )
    table = (first + second).reshape(Q, row_count, Q, col_count)
    return jnp.transpose(table, (1, 3, 0, 2)).reshape(row_count * col_count, Q, Q)


def shards(couplings, fields, tokens, seq_weights, block_cols, block_count):
    rows_here, slot_count = block_cols.shape
    positions, seq_here = tokens.shape
    blocks_all = positions // B
    owner_index = lax.axis_index("pos")
    total_seqs = seq_here * lax.axis_size("seq")
    states = jnp.arange(Q, dtype=jnp.int32)
    onehot = (
        tokens.reshape(blocks_all, B, seq_here)[:, None, :, :] == states[None, :, None, None]
    ).astype(jnp.bfloat16)
    block_shape = (Q, B, seq_here)
    partials = jnp.zeros((blocks_all, Q, B, seq_here), jnp.float32)
    local_row = 0
    row_block = owner_index * rows_here + local_row
    hot_row = lax.dynamic_index_in_dim(onehot, row_block, 0, keepdims=False)
    for slot_index in range(slot_count):
        column = block_cols[local_row, slot_index]
        is_live = slot_index < block_count[local_row]
        matrix = pair_matrix(couplings[local_row, slot_index], Q, B)
        hot_col = lax.dynamic_index_in_dim(onehot, column, 0, keepdims=False)

        def contribute(matrix=matrix, hot_col=hot_col, hot_row=hot_row):
            own_term = jnp.dot(
                matrix, hot_col.reshape(Q * B, seq_here), preferred_element_type=jnp.float32
            )
            across = lax.dot_general(
                matrix,
                hot_row.reshape(Q * B, seq_here),
                (((0,), (0,)), ((), ())),
                preferred_element_type=jnp.float32,
            )
            return (own_term.reshape(block_shape), across.reshape(block_shape))

        own_term, across = gated(is_live, contribute)
        partials = add_block(partials, row_block, own_term)
        partials = add_block(partials, column, across)
    summed = lax.psum_scatter(
        partials.astype(jnp.bfloat16), "pos", scatter_dimension=0, tiled=True
    ).astype(jnp.float32)
    logits = summed + fields[..., None]
    softmax_probs = jax.nn.softmax(logits, axis=1)
    own_rows = lax.dynamic_slice_in_dim(onehot, owner_index * rows_here, rows_here, 0).astype(
        jnp.float32
    )
    seq_scale = seq_weights.astype(jnp.float32) / total_seqs
    residual = ((softmax_probs - own_rows) * seq_scale).astype(jnp.bfloat16)
    grad_fields = lax.psum(jnp.sum(residual.astype(jnp.float32), axis=3), "seq")
    residual_all = lax.all_gather(residual, "pos", axis=0, tiled=True)
    share_len = couplings.shape[-1] // lax.axis_size("seq")
    slot_grads = []
    local_row = 0
    row_block = owner_index * rows_here + local_row
    hot_row = lax.dynamic_index_in_dim(onehot, row_block, 0, keepdims=False)
    res_row = lax.dynamic_index_in_dim(residual_all, row_block, 0, keepdims=False)
    for slot_index in range(slot_count):
        column = block_cols[local_row, slot_index]
        is_live = slot_index < block_count[local_row]
        hot_col = lax.dynamic_index_in_dim(onehot, column, 0, keepdims=False)
        res_col = lax.dynamic_index_in_dim(residual_all, column, 0, keepdims=False)

        def slot_term(
            start,
            count,
            hot_row=hot_row,
            res_row=res_row,
            hot_col=hot_col,
            res_col=res_col,
            is_live=is_live,
        ):

            def compute():
                return (pair_rows(res_row, hot_row, res_col, hot_col, count // B, B),)

            (term,) = gated(is_live, compute)
            return term

        share = lax.psum_scatter(
            slot_term(jnp.int32(0), lax.axis_size("seq") * share_len),
            "seq",
            scatter_dimension=0,
            tiled=True,
        )
        slot_grads.append(jnp.transpose(share, (1, 2, 0)))
    grad_couplings = jnp.stack(slot_grads).reshape(rows_here, slot_count, Q, Q, share_len)
    return (grad_couplings, grad_fields)


def relay(w, table):
    pairs, lanes = B // 2, 2 * B

    def move(step, carry):
        for sub in range(3):
            a = step * 3 + sub
            blocks = w[0, a].reshape(Q, pairs, lanes)
            for b in range(Q):
                table[pl.ds(pl.multiple_of(a * pairs, pairs), pairs), b * lanes : (b + 1) * lanes] = blocks[b]
        return carry

    lax.fori_loop(0, Q // 3, move, 0)


def own_kernel(cols, count, w, tok, own, table, hot_col, acc_own):
    slot = pl.program_id(0)
    seqs = tok.shape[1]
    pairs, lanes = B // 2, 2 * B

    @pl.when(slot == 0)
    def _():
        acc_own[...] = jnp.zeros_like(acc_own)
        hot_col[...] = jnp.zeros_like(hot_col)

    @pl.when(slot < count[0])
    def _():
        relay(w, table)
        ids = tok[pl.ds(pl.multiple_of(cols[0, slot] * B, B), B), :]
        for b in range(Q):
            hot = jnp.where(ids == b, 1.0, 0.0).astype(jnp.bfloat16)
            hot_col[b * lanes : b * lanes + B, :seqs] = hot
            hot_col[b * lanes + B : (b + 1) * lanes, seqs:] = hot
        acc_own[...] += jnp.dot(table[...], hot_col[...], preferred_element_type=jnp.float32)

    @pl.when(slot == pl.num_programs(0) - 1)
    def _():
        for odd in range(2):
            own[pl.ds(odd, Q * pairs, stride=2), :] = acc_own[:, odd * seqs : (odd + 1) * seqs]


def across_kernel(cols, count, w, tok, near, mid, far, table, hot_own, acc):
    slot = pl.program_id(0)
    seqs = tok.shape[1]
    pairs = B // 2
    lanes = 2 * B
    here = lax.axis_index("pos")
    lane = lax.broadcasted_iota(jnp.int32, (seqs, lanes), 1)

    @pl.when(slot == 0)
    def _():
        acc[...] = jnp.zeros_like(acc)
        table[Q * pairs :, :] = jnp.zeros((table.shape[0] - Q * pairs, table.shape[1]), table.dtype)
        for odd in range(2):
            ids = tok[pl.ds(here * B + odd, pairs, stride=2), :].astype(jnp.float32)
            ids = jnp.concatenate([ids] * 4, axis=0).T
            for tile in range(table.shape[0] // lanes):
                state = (4 * tile + lane // pairs).astype(jnp.float32)
                hot_own[odd * seqs : (odd + 1) * seqs, tile * lanes : (tile + 1) * lanes] = jnp.where(
                    ids == state, 1.0, 0.0
                ).astype(jnp.bfloat16)

    @pl.when(slot < count[0])
    def _():
        role = lax.bitwise_xor(cols[0, slot], here)
        relay(w, table)
        for b in range(0, Q, 2):
            width = 2 if b + 1 < Q else 1
            part = jnp.dot(
                hot_own[...],
                table[:, b * lanes : (b + width) * lanes],
                preferred_element_type=jnp.float32,
            )
            top0, low0 = part[:seqs, :lanes], part[seqs:, :lanes]
            if width == 2:
                top1, low1 = part[:seqs, lanes:], part[seqs:, lanes:]
            else:
                top1, low1 = top0, low0
            both = jnp.where(lane < B, top0, low1) + pltpu.roll(jnp.where(lane < B, top1, low0), B, 1)
            rows = slice(b * B, (b + width) * B)
            acc[role, rows, :] += both.T[: width * B, :]

    @pl.when(slot == pl.num_programs(0) - 1)
    def _():
        near[...] = acc[1].astype(jnp.bfloat16)
        mid[...] = acc[2].astype(jnp.bfloat16)
        far[...] = acc[3].astype(jnp.bfloat16)


def forward_call(kernel, name, outs, scratch, couplings, tokens, block_cols, block_count):
    slots = couplings.shape[1]
    positions, seqs = tokens.shape
    rows = Q * B
    smem = pl.BlockSpec(memory_space=pltpu.SMEM)
    return pl.pallas_call(
        kernel,
        grid=(slots,),
        in_specs=[
            smem,
            smem,
            pl.BlockSpec((1, Q, Q, B * B), lambda k: (k, 0, 0, 0)),
            pl.BlockSpec((positions, seqs), lambda k: (0, 0)),
        ],
        out_specs=[pl.BlockSpec((rows, seqs), lambda k: (0, 0))] * len(outs),
        out_shape=[jax.ShapeDtypeStruct((rows, seqs), dtype) for dtype in outs],
        scratch_shapes=scratch,
        compiler_params=pltpu.CompilerParams(vmem_limit_bytes=VMEM_BYTES),
        cost_estimate=pl.CostEstimate(
            flops=2 * 4 * slots * rows * rows * seqs, bytes_accessed=2 * couplings.size, transcendentals=0
        ),
        name=name,
    )(block_cols, block_count, couplings.reshape(slots, Q, Q, B * B), tokens)


def across_terms(couplings, tokens, block_cols, block_count):
    seqs, pairs, lanes = tokens.shape[1], B // 2, 2 * B
    depth = -(-Q * pairs // lanes) * lanes
    scratch = [
        pltpu.VMEM((depth, Q * lanes), jnp.bfloat16),
        pltpu.VMEM((2 * seqs, depth), jnp.bfloat16),
        pltpu.VMEM((4, Q * B, seqs), jnp.float32),
    ]
    return forward_call(
        across_kernel, "across", [jnp.bfloat16] * 3, scratch, couplings, tokens, block_cols, block_count
    )


def own_terms(couplings, tokens, block_cols, block_count):
    seqs, pairs, lanes = tokens.shape[1], B // 2, 2 * B
    scratch = [
        pltpu.VMEM((Q * pairs, Q * lanes), jnp.bfloat16),
        pltpu.VMEM((Q * lanes, 2 * seqs), jnp.bfloat16),
        pltpu.VMEM((Q * pairs, 2 * seqs), jnp.float32),
    ]
    (own,) = forward_call(
        own_kernel, "own", [jnp.float32], scratch, couplings, tokens, block_cols, block_count
    )
    return own


def residual_kernel(total, own, first, second, fields, tok, weights, res):
    here = lax.axis_index("pos")
    step = 16
    scale = weights[...].astype(jnp.float32) / total
    field = fields[0].T
    for start in range(0, B, step):
        ids = tok[pl.ds(pl.multiple_of(here * B + start, step), step), :]
        logits = []
        for a in range(Q):
            rows = slice(a * B + start, a * B + start + step)
            terms = first[rows, :].astype(jnp.float32) + second[rows, :].astype(jnp.float32)
            logits.append(own[rows, :] + terms + field[start : start + step, a : a + 1])
        top = logits[0]
        for a in range(1, Q):
            top = jnp.maximum(top, logits[a])
        powers = [jnp.exp(value - top) for value in logits]
        norm = powers[0]
        for a in range(1, Q):
            norm = norm + powers[a]
        inverse = 1.0 / norm
        for a in range(Q):
            probs = powers[a] * inverse
            res[a * B + start : a * B + start + step, :] = (
                (probs - jnp.where(ids == a, 1.0, 0.0)) * scale
            ).astype(jnp.bfloat16)


def residuals(own, first, second, fields, tokens, seq_weights, total):
    rows, seqs = own.shape
    return pl.pallas_call(
        functools.partial(residual_kernel, total),
        out_shape=jax.ShapeDtypeStruct((rows, seqs), jnp.bfloat16),
        compiler_params=pltpu.CompilerParams(vmem_limit_bytes=VMEM_BYTES),
        cost_estimate=pl.CostEstimate(
            flops=20 * rows * seqs, bytes_accessed=10 * rows * seqs, transcendentals=rows * seqs
        ),
        name="residuals",
    )(own, first, second, fields, tokens, seq_weights.reshape(1, seqs))


def prepare_kernel(shards_in, *refs):
    toks, mine = refs[:shards_in], refs[shards_in : 2 * shards_in]
    left, sums, spread = refs[2 * shards_in :]
    here, share = lax.axis_index("pos"), lax.axis_index("seq")
    seqs = toks[0].shape[1]
    depth = shards_in * seqs
    part = left.shape[0] // Q
    half = part // 2
    ones = jnp.ones((8, seqs), jnp.bfloat16)
    total = sum(
        lax.dot_general(ones, piece[...], (((1,), (1,)), ((), ())), preferred_element_type=jnp.float32)
        for piece in mine
    )
    for a in range(Q):
        sums[a] = total[:1, a * B : (a + 1) * B]
    for n in range(shards_in):
        span = slice(n * seqs, (n + 1) * seqs)
        over = slice(depth + n * seqs, depth + (n + 1) * seqs)
        for a in range(Q):
            start = pl.multiple_of(a * B + share * part, part)
            spread[a * part : (a + 1) * part, :] = mine[n][pl.ds(start, part), :].astype(jnp.float32)
        start = here * B + share * part
        ids = jnp.concatenate([toks[n][pl.ds(start + odd, half, stride=2), :] for odd in range(2)], axis=0)
        for a in range(Q):
            piece = jnp.concatenate(
                [spread[pl.ds(a * part + odd, half, stride=2), :] for odd in range(2)], axis=0
            )
            left[a * part : (a + 1) * part, span] = piece.astype(jnp.bfloat16)
            left[a * part : (a + 1) * part, over] = jnp.where(ids == a, 1.0, 0.0).astype(jnp.bfloat16)


def prepare(toks, mine):
    rows, seqs = mine[0].shape
    shards_in = len(toks)
    part = B // lax.axis_size("seq")
    return pl.pallas_call(
        functools.partial(prepare_kernel, shards_in),
        out_shape=[
            jax.ShapeDtypeStruct((Q * part, 2 * shards_in * seqs), jnp.bfloat16),
            jax.ShapeDtypeStruct((Q, 1, B), jnp.float32),
        ],
        scratch_shapes=[pltpu.VMEM((Q * part, seqs), jnp.float32)],
        compiler_params=pltpu.CompilerParams(vmem_limit_bytes=VMEM_BYTES),
        cost_estimate=pl.CostEstimate(
            flops=16 * rows * seqs * shards_in, bytes_accessed=4 * rows * seqs * shards_in, transcendentals=0
        ),
        name="prepare",
    )(*toks, *mine)


def gradient_kernel(roles, shards_in, opening, cols, count, left_from, *refs):
    toks, others = refs[:shards_in], refs[shards_in : 2 * shards_in]
    out, left, right, ids, tiles, sems, arrived = refs[-7:]
    here = lax.axis_index("pos")
    slots = out.shape[0]
    seqs = ids.shape[2]
    depth = shards_in * seqs
    part = left.shape[0] // Q
    half = part // 2
    lanes = 2 * B
    dims = (((1,), (1,)), ((), ()))
    if opening:
        tiles[...] = jnp.zeros_like(tiles)
        for slot in range(slots):

            @pl.when(slot >= count[0])
            def _(slot=slot):
                copy = pltpu.make_async_copy(tiles, out.at[slot], sems.at[slot, 0])
                copy.start()
                copy.wait()

    block = lax.bitwise_xor(here, jnp.where(jnp.logical_or(here == 0, here == 3), roles[0], roles[1]))
    wanted = [jnp.logical_and(slot < count[0], cols[0, slot] == block) for slot in range(slots)]
    needed = wanted[0]
    for flag in wanted[1:]:
        needed = jnp.logical_or(needed, flag)

    @pl.when(needed)
    def _():
        rows_of = pl.ds(pl.multiple_of(block * B, B), B)
        fetches = [
            pltpu.make_async_copy(toks[n].at[rows_of], ids.at[n], arrived.at[n]) for n in range(shards_in)
        ]
        fetches += [pltpu.make_async_copy(left_from, left, arrived.at[2 * shards_in])]
        fetches += [
            pltpu.make_async_copy(
                others[n], right.at[:, pl.ds(depth + n * seqs, seqs)], arrived.at[shards_in + n]
            )
            for n in range(shards_in)
        ]
        for fetch in fetches:
            fetch.start()
        for n in range(shards_in):
            fetches[n].wait()
            span = slice(n * seqs, (n + 1) * seqs)
            states = ids[n]
            for b in range(Q):
                right[b * B : (b + 1) * B, span] = jnp.where(states == b, 1.0, 0.0).astype(jnp.bfloat16)
        for fetch in fetches[shards_in:]:
            fetch.wait()
        lane = lax.broadcasted_iota(jnp.int32, (half, lanes), 1)
        for b in range(0, Q, 4):
            width = min(4, Q - b)
            rows = lax.dot_general(
                left[...], right[b * B : (b + width) * B, :], dims, preferred_element_type=jnp.float32
            )
            if width * B % lanes:
                rows = jnp.concatenate([rows, rows], axis=1)
            for a in range(Q):
                for pair in range(0, width, 2):
                    columns = slice(pair * B, pair * B + lanes)
                    even = rows[a * part : a * part + half, columns]
                    odd = rows[a * part + half : (a + 1) * part, columns]
                    at = (b + pair) * half
                    tiles[a, at : at + half, :] = jnp.where(lane < B, even, pltpu.roll(odd, B, 1))
                    if pair + 1 < width:
                        tiles[a, at + half : at + 2 * half, :] = jnp.where(lane < B, pltpu.roll(even, B, 1), odd)
            for slot in range(slots):

                @pl.when(wanted[slot])
                def _(slot=slot, b=b, width=width):
                    group = pl.ds(b * half, width * half)
                    pltpu.make_async_copy(tiles.at[:, group], out.at[slot, :, group], sems.at[slot, b // 4]).start()

        for b in range(0, Q, 4):
            for slot in range(slots):

                @pl.when(wanted[slot])
                def _(slot=slot, b=b):
                    group = pl.ds(b * half, min(4, Q - b) * half)
                    pltpu.make_async_copy(tiles.at[:, group], out.at[slot, :, group], sems.at[slot, b // 4]).wait()


def gradient(roles, block_cols, block_count, left, toks, others, done):
    slots = block_cols.shape[1]
    rows, seqs = others[0].shape
    shards_in = len(toks)
    part = B // lax.axis_size("seq")
    smem = pl.BlockSpec(memory_space=pltpu.SMEM)
    anywhere = pl.BlockSpec(memory_space=pl.ANY)
    operands = [block_cols, block_count, left, *toks, *others]
    specs = [smem, smem] + [anywhere] * (1 + 2 * shards_in)
    aliases = {}
    if done is not None:
        aliases = {len(operands): 0}
        operands.append(done)
        specs.append(anywhere)
    height = Q * part // 2
    return pl.pallas_call(
        functools.partial(gradient_kernel, roles, shards_in, done is None),
        in_specs=specs,
        out_specs=anywhere,
        out_shape=jax.ShapeDtypeStruct((slots, Q, height, 2 * B), jnp.float32),
        input_output_aliases=aliases,
        scratch_shapes=[
            pltpu.VMEM((Q * part, 2 * shards_in * seqs), jnp.bfloat16),
            pltpu.VMEM((rows, 2 * shards_in * seqs), jnp.bfloat16),
            pltpu.VMEM((shards_in, B, seqs), jnp.int32),
            pltpu.VMEM((Q, height, 2 * B), jnp.float32),
            pltpu.SemaphoreType.DMA((slots, -(-Q // 4))),
            pltpu.SemaphoreType.DMA((2 * shards_in + 1,)),
        ],
        compiler_params=pltpu.CompilerParams(vmem_limit_bytes=VMEM_BYTES),
        cost_estimate=pl.CostEstimate(
            flops=4 * Q * part * rows * shards_in * seqs,
            bytes_accessed=4 * Q * height * 2 * B + 4 * rows * seqs * shards_in,
            transcendentals=0,
        ),
        name="gradient",
    )(*operands)


def partner(bits, axis):
    return [(i, i ^ bits) for i in range(lax.axis_size(axis))]


def exchanged(value, bits, axis):
    return lax.ppermute(value, axis, partner(bits, axis))


def over_seq(value):
    along = exchanged(value, 2, "seq")
    return [value, along, exchanged(value, 1, "seq"), exchanged(along, 1, "seq")]


def shards_four(couplings, fields, tokens, seq_weights, block_cols, block_count):
    total_seqs = tokens.shape[1] * lax.axis_size("seq")
    tok_along, tok_core = exchanged(tokens, 2, "seq"), exchanged(tokens, 1, "seq")
    near, mid, far = across_terms(couplings, tokens, block_cols, block_count)
    near, mid, far, tok_along, tok_core = lax.optimization_barrier((near, mid, far, tok_along, tok_core))
    pair = far.astype(jnp.float32) + exchanged(mid, 1, "pos").astype(jnp.float32)
    second = exchanged(near, 1, "pos")
    first = exchanged(pair.astype(jnp.bfloat16), 3, "pos")
    toks = [tokens, tok_along, tok_core, exchanged(tok_along, 1, "seq")]
    own = own_terms(couplings, tokens, block_cols, block_count)
    own, toks = lax.optimization_barrier((own, toks))
    res = residuals(own, first, second, fields, tokens, seq_weights, total_seqs)
    steady = lax.optimization_barrier
    along, near_res, far_res = exchanged(res, 2, "seq"), exchanged(res, 1, "pos"), exchanged(res, 3, "pos")
    near_res, along = steady((near_res, along))
    near_along = exchanged(near_res, 2, "seq")
    left, sums = prepare(toks, [res, along, exchanged(res, 1, "seq"), exchanged(along, 1, "seq")])
    mid_res = exchanged(far_res, 1, "pos")
    far_along = exchanged(far_res, 2, "seq")
    mid_res, near_along, left = steady((mid_res, near_along, left))
    mid_along = exchanged(mid_res, 2, "seq")
    nears = [near_res, near_along, exchanged(near_res, 1, "seq"), exchanged(near_along, 1, "seq")]
    grad = gradient((1, 1), block_cols, block_count, left, toks, nears, None)
    fars = [far_res, far_along, exchanged(far_res, 1, "seq"), exchanged(far_along, 1, "seq")]
    grad = gradient((3, 3), block_cols, block_count, left, toks, fars, grad)
    mid_core = exchanged(mid_res, 1, "seq")
    mid_along, grad, mid_core = steady((mid_along, grad, mid_core))
    mids = [mid_res, mid_along, mid_core, exchanged(mid_along, 1, "seq")]
    grad = gradient((2, 2), block_cols, block_count, left, toks, mids, grad)
    share_len = couplings.shape[-1] // lax.axis_size("seq")
    return (grad.reshape(1, couplings.shape[1], Q, Q, share_len), sums.reshape(1, Q, B))


def solution(mesh):
    placed = (
        P(("grp", "pos"), None, None, None, None),
        P(("grp", "pos"), None, None),
        P("grp", "seq"),
        P(("grp", "seq")),
        P(("grp", "pos"), None),
        P(("grp", "pos")),
    )
    return jax.shard_map(
        shards_four if mesh.shape["pos"] == 4 and mesh.shape["seq"] == 4 else shards,
        mesh=mesh,
        in_specs=placed,
        out_specs=(P(("grp", "pos"), None, None, None, "seq"), P(("grp", "pos"), None, None)),
        check_vma=False,
    )
```

```python
import functools

import jax
import jax.numpy as jnp
from jax import lax
from jax.experimental import pallas as pl
from jax.experimental.pallas import tpu as pltpu
from jax.sharding import PartitionSpec as P

Q = 21
B = 64
VMEM_BYTES = 40 * 1024 * 1024
ACROSS_VMEM_BYTES = 56 * 1024 * 1024
OWN_VMEM_BYTES = 50 * 1024 * 1024


def add_block(total, index, block):
    current = lax.dynamic_index_in_dim(total, index, 0, keepdims=False)
    return lax.dynamic_update_index_in_dim(total, current + block, index, 0)


def gated(is_live, compute):
    values = compute()
    switch = is_live.astype(jnp.float32)
    return tuple((value * switch for value in values))


def pair_matrix(coupling, states, width):
    square = coupling.reshape(states, states, width, width)
    return jnp.transpose(square, (0, 2, 1, 3)).reshape(states * width, states * width)


def pair_rows(res_row, hot_row, res_col, hot_col, row_count, col_count):
    seq_len = res_row.shape[-1]
    dims = (((1,), (1,)), ((), ()))
    first = lax.dot_general(
        res_row.reshape(Q * row_count, seq_len),
        hot_col.reshape(Q * col_count, seq_len),
        dims,
        preferred_element_type=jnp.float32,
    )
    second = lax.dot_general(
        hot_row.reshape(Q * row_count, seq_len),
        res_col.reshape(Q * col_count, seq_len),
        dims,
        preferred_element_type=jnp.float32,
    )
    table = (first + second).reshape(Q, row_count, Q, col_count)
    return jnp.transpose(table, (1, 3, 0, 2)).reshape(row_count * col_count, Q, Q)


def shards(couplings, fields, tokens, seq_weights, block_cols, block_count):
    rows_here, slot_count = block_cols.shape
    positions, seq_here = tokens.shape
    blocks_all = positions // B
    owner_index = lax.axis_index("pos")
    total_seqs = seq_here * lax.axis_size("seq")
    states = jnp.arange(Q, dtype=jnp.int32)
    onehot = (
        tokens.reshape(blocks_all, B, seq_here)[:, None, :, :] == states[None, :, None, None]
    ).astype(jnp.bfloat16)
    block_shape = (Q, B, seq_here)
    partials = jnp.zeros((blocks_all, Q, B, seq_here), jnp.float32)
    local_row = 0
    row_block = owner_index * rows_here + local_row
    hot_row = lax.dynamic_index_in_dim(onehot, row_block, 0, keepdims=False)
    for slot_index in range(slot_count):
        column = block_cols[local_row, slot_index]
        is_live = slot_index < block_count[local_row]
        matrix = pair_matrix(couplings[local_row, slot_index], Q, B)
        hot_col = lax.dynamic_index_in_dim(onehot, column, 0, keepdims=False)

        def contribute(matrix=matrix, hot_col=hot_col, hot_row=hot_row):
            own_term = jnp.dot(
                matrix, hot_col.reshape(Q * B, seq_here), preferred_element_type=jnp.float32
            )
            across = lax.dot_general(
                matrix,
                hot_row.reshape(Q * B, seq_here),
                (((0,), (0,)), ((), ())),
                preferred_element_type=jnp.float32,
            )
            return (own_term.reshape(block_shape), across.reshape(block_shape))

        own_term, across = gated(is_live, contribute)
        partials = add_block(partials, row_block, own_term)
        partials = add_block(partials, column, across)
    summed = lax.psum_scatter(
        partials.astype(jnp.bfloat16), "pos", scatter_dimension=0, tiled=True
    ).astype(jnp.float32)
    logits = summed + fields[..., None]
    softmax_probs = jax.nn.softmax(logits, axis=1)
    own_rows = lax.dynamic_slice_in_dim(onehot, owner_index * rows_here, rows_here, 0).astype(
        jnp.float32
    )
    seq_scale = seq_weights.astype(jnp.float32) / total_seqs
    residual = ((softmax_probs - own_rows) * seq_scale).astype(jnp.bfloat16)
    grad_fields = lax.psum(jnp.sum(residual.astype(jnp.float32), axis=3), "seq")
    residual_all = lax.all_gather(residual, "pos", axis=0, tiled=True)
    share_len = couplings.shape[-1] // lax.axis_size("seq")
    slot_grads = []
    local_row = 0
    row_block = owner_index * rows_here + local_row
    hot_row = lax.dynamic_index_in_dim(onehot, row_block, 0, keepdims=False)
    res_row = lax.dynamic_index_in_dim(residual_all, row_block, 0, keepdims=False)
    for slot_index in range(slot_count):
        column = block_cols[local_row, slot_index]
        is_live = slot_index < block_count[local_row]
        hot_col = lax.dynamic_index_in_dim(onehot, column, 0, keepdims=False)
        res_col = lax.dynamic_index_in_dim(residual_all, column, 0, keepdims=False)

        def slot_term(
            start,
            count,
            hot_row=hot_row,
            res_row=res_row,
            hot_col=hot_col,
            res_col=res_col,
            is_live=is_live,
        ):

            def compute():
                return (pair_rows(res_row, hot_row, res_col, hot_col, count // B, B),)

            (term,) = gated(is_live, compute)
            return term

        share = lax.psum_scatter(
            slot_term(jnp.int32(0), lax.axis_size("seq") * share_len),
            "seq",
            scatter_dimension=0,
            tiled=True,
        )
        slot_grads.append(jnp.transpose(share, (1, 2, 0)))
    grad_couplings = jnp.stack(slot_grads).reshape(rows_here, slot_count, Q, Q, share_len)
    return (grad_couplings, grad_fields)


PIECES = 3


def in_vmem(value):
    return pltpu.with_memory_space_constraint(value, pltpu.VMEM)


def fetch(w, held, arrived, slot, piece):
    states = pl.ds(piece * (Q // PIECES), Q // PIECES)
    return pltpu.make_async_copy(w.at[slot, states], held.at[slot, states], arrived.at[slot, piece])


def fetch_live(w, held, arrived, count):
    for slot in range(w.shape[0]):

        @pl.when(slot < count[0])
        def _(slot=slot):
            for piece in range(PIECES):
                fetch(w, held, arrived, slot, piece).start()


def relay(w, held, arrived, slot, table):
    pairs, lanes = B // 2, 2 * B

    def move(piece, carry):
        fetch(w, held, arrived, slot, piece).wait()
        for sub in range(Q // PIECES):
            a = piece * (Q // PIECES) + sub
            blocks = held[slot, a].reshape(Q, pairs, lanes)
            for b in range(Q):
                table[pl.ds(pl.multiple_of(a * pairs, pairs), pairs), b * lanes : (b + 1) * lanes] = blocks[b]
        return carry

    lax.fori_loop(0, PIECES, move, 0)


def own_kernel(cols, count, w, tok, own, held, arrived, table, hot_col, acc_own):
    slot = pl.program_id(0)
    seqs = tok.shape[1]
    pairs, lanes = B // 2, 2 * B

    @pl.when(slot == 0)
    def _():
        fetch_live(w, held, arrived, count)
        acc_own[...] = jnp.zeros_like(acc_own)
        hot_col[...] = jnp.zeros_like(hot_col)

    @pl.when(slot < count[0])
    def _():
        relay(w, held, arrived, slot, table)
        ids = tok[pl.ds(pl.multiple_of(cols[0, slot] * B, B), B), :]
        for b in range(Q):
            hot = jnp.where(ids == b, 1.0, 0.0).astype(jnp.bfloat16)
            hot_col[b * lanes : b * lanes + B, :seqs] = hot
            hot_col[b * lanes + B : (b + 1) * lanes, seqs:] = hot
        acc_own[...] += jnp.dot(table[...], hot_col[...], preferred_element_type=jnp.float32)

    @pl.when(slot == pl.num_programs(0) - 1)
    def _():
        for odd in range(2):
            own[pl.ds(odd, Q * pairs, stride=2), :] = acc_own[:, odd * seqs : (odd + 1) * seqs]


def across_kernel(cols, count, w, tok, near, mid, far, held, arrived, table, hot_own, acc):
    slot = pl.program_id(0)
    seqs = tok.shape[1]
    pairs = B // 2
    lanes = 2 * B
    here = lax.axis_index("pos")
    lane = lax.broadcasted_iota(jnp.int32, (seqs, lanes), 1)

    @pl.when(slot == 0)
    def _():
        fetch_live(w, held, arrived, count)
        acc[...] = jnp.zeros_like(acc)
        table[Q * pairs :, :] = jnp.zeros((table.shape[0] - Q * pairs, table.shape[1]), table.dtype)
        for odd in range(2):
            ids = tok[pl.ds(here * B + odd, pairs, stride=2), :].astype(jnp.float32)
            ids = jnp.concatenate([ids] * 4, axis=0).T
            for tile in range(table.shape[0] // lanes):
                state = (4 * tile + lane // pairs).astype(jnp.float32)
                hot_own[odd * seqs : (odd + 1) * seqs, tile * lanes : (tile + 1) * lanes] = jnp.where(
                    ids == state, 1.0, 0.0
                ).astype(jnp.bfloat16)

    @pl.when(slot < count[0])
    def _():
        role = lax.bitwise_xor(cols[0, slot], here)
        relay(w, held, arrived, slot, table)
        for b in range(0, Q, 2):
            width = 2 if b + 1 < Q else 1
            part = jnp.dot(
                hot_own[...],
                table[:, b * lanes : (b + width) * lanes],
                preferred_element_type=jnp.float32,
            )
            top0, low0 = part[:seqs, :lanes], part[seqs:, :lanes]
            if width == 2:
                top1, low1 = part[:seqs, lanes:], part[seqs:, lanes:]
            else:
                top1, low1 = top0, low0
            both = jnp.where(lane < B, top0, low1) + pltpu.roll(jnp.where(lane < B, top1, low0), B, 1)
            rows = slice(b * B, (b + width) * B)
            acc[role, rows, :] += both.T[: width * B, :]

    @pl.when(slot == pl.num_programs(0) - 1)
    def _():
        near[...] = acc[1].astype(jnp.bfloat16)
        mid[...] = acc[2].astype(jnp.bfloat16)
        far[...] = acc[3].astype(jnp.bfloat16)


def forward_call(kernel, name, outs, vmem_bytes, scratch, couplings, tokens, block_cols, block_count):
    slots = couplings.shape[1]
    positions, seqs = tokens.shape
    rows = Q * B
    smem = pl.BlockSpec(memory_space=pltpu.SMEM)
    return pl.pallas_call(
        kernel,
        grid=(slots,),
        in_specs=[
            smem,
            smem,
            pl.BlockSpec(memory_space=pl.ANY),
            pl.BlockSpec((positions, seqs), lambda k: (0, 0)),
        ],
        out_specs=[pl.BlockSpec((rows, seqs), lambda k: (0, 0))] * len(outs),
        out_shape=[jax.ShapeDtypeStruct((rows, seqs), dtype) for dtype in outs],
        scratch_shapes=[
            pltpu.VMEM((slots, Q, Q, B * B), couplings.dtype),
            pltpu.SemaphoreType.DMA((slots, PIECES)),
            *scratch,
        ],
        compiler_params=pltpu.CompilerParams(vmem_limit_bytes=vmem_bytes),
        cost_estimate=pl.CostEstimate(
            flops=2 * 4 * slots * rows * rows * seqs, bytes_accessed=2 * couplings.size, transcendentals=0
        ),
        name=name,
    )(block_cols, block_count, couplings.reshape(slots, Q, Q, B * B), tokens)


def across_terms(couplings, tokens, block_cols, block_count):
    seqs, pairs, lanes = tokens.shape[1], B // 2, 2 * B
    depth = -(-Q * pairs // lanes) * lanes
    scratch = [
        pltpu.VMEM((depth, Q * lanes), jnp.bfloat16),
        pltpu.VMEM((2 * seqs, depth), jnp.bfloat16),
        pltpu.VMEM((4, Q * B, seqs), jnp.float32),
    ]
    return forward_call(
        across_kernel, "across", [jnp.bfloat16] * 3, ACROSS_VMEM_BYTES, scratch, couplings, tokens, block_cols, block_count
    )


def own_terms(couplings, tokens, block_cols, block_count):
    seqs, pairs, lanes = tokens.shape[1], B // 2, 2 * B
    scratch = [
        pltpu.VMEM((Q * pairs, Q * lanes), jnp.bfloat16),
        pltpu.VMEM((Q * lanes, 2 * seqs), jnp.bfloat16),
        pltpu.VMEM((Q * pairs, 2 * seqs), jnp.float32),
    ]
    (own,) = forward_call(
        own_kernel, "own", [jnp.float32], OWN_VMEM_BYTES, scratch, couplings, tokens, block_cols, block_count
    )
    return own


def pair_kernel(left, right, out):
    out[...] = (left[...].astype(jnp.float32) + right[...].astype(jnp.float32)).astype(jnp.bfloat16)


def pair_sum(left, right):
    return pl.pallas_call(
        pair_kernel,
        out_shape=jax.ShapeDtypeStruct(left.shape, jnp.bfloat16),
        compiler_params=pltpu.CompilerParams(vmem_limit_bytes=VMEM_BYTES),
        cost_estimate=pl.CostEstimate(flops=left.size, bytes_accessed=6 * left.size, transcendentals=0),
        name="pair_sum",
    )(in_vmem(left), in_vmem(right))


def residual_kernel(total, own, first, second, fields, tok, weights, res):
    here = lax.axis_index("pos")
    step = 16
    scale = weights[...].astype(jnp.float32) / total
    field = fields[0].T
    for start in range(0, B, step):
        ids = tok[pl.ds(pl.multiple_of(here * B + start, step), step), :]
        logits = []
        for a in range(Q):
            rows = slice(a * B + start, a * B + start + step)
            terms = first[rows, :].astype(jnp.float32) + second[rows, :].astype(jnp.float32)
            logits.append(own[rows, :] + terms + field[start : start + step, a : a + 1])
        top = logits[0]
        for a in range(1, Q):
            top = jnp.maximum(top, logits[a])
        powers = [jnp.exp(value - top) for value in logits]
        norm = powers[0]
        for a in range(1, Q):
            norm = norm + powers[a]
        inverse = 1.0 / norm
        for a in range(Q):
            probs = powers[a] * inverse
            res[a * B + start : a * B + start + step, :] = (
                (probs - jnp.where(ids == a, 1.0, 0.0)) * scale
            ).astype(jnp.bfloat16)


def residuals(own, first, second, fields, tokens, seq_weights, total):
    rows, seqs = own.shape
    return pl.pallas_call(
        functools.partial(residual_kernel, total),
        out_shape=jax.ShapeDtypeStruct((rows, seqs), jnp.bfloat16),
        compiler_params=pltpu.CompilerParams(vmem_limit_bytes=VMEM_BYTES),
        cost_estimate=pl.CostEstimate(
            flops=20 * rows * seqs, bytes_accessed=10 * rows * seqs, transcendentals=rows * seqs
        ),
        name="residuals",
    )(own, first, second, fields, tokens, seq_weights.reshape(1, seqs))


def prepare_kernel(shards_in, *refs):
    toks, mine = refs[:shards_in], refs[shards_in : 2 * shards_in]
    left, sums, spread = refs[2 * shards_in :]
    here, share = lax.axis_index("pos"), lax.axis_index("seq")
    seqs = toks[0].shape[1]
    depth = shards_in * seqs
    part = left.shape[0] // Q
    half = part // 2
    ones = jnp.ones((8, seqs), jnp.bfloat16)
    total = sum(
        lax.dot_general(ones, piece[...], (((1,), (1,)), ((), ())), preferred_element_type=jnp.float32)
        for piece in mine
    )
    for a in range(Q):
        sums[a] = total[:1, a * B : (a + 1) * B]
    for n in range(shards_in):
        span = slice(n * seqs, (n + 1) * seqs)
        over = slice(depth + n * seqs, depth + (n + 1) * seqs)
        for a in range(Q):
            start = pl.multiple_of(a * B + share * part, part)
            spread[a * part : (a + 1) * part, :] = mine[n][pl.ds(start, part), :].astype(jnp.float32)
        start = here * B + share * part
        ids = jnp.concatenate([toks[n][pl.ds(start + odd, half, stride=2), :] for odd in range(2)], axis=0)
        for a in range(Q):
            piece = jnp.concatenate(
                [spread[pl.ds(a * part + odd, half, stride=2), :] for odd in range(2)], axis=0
            )
            left[a * part : (a + 1) * part, span] = piece.astype(jnp.bfloat16)
            left[a * part : (a + 1) * part, over] = jnp.where(ids == a, 1.0, 0.0).astype(jnp.bfloat16)


def prepare(toks, mine):
    rows, seqs = mine[0].shape
    shards_in = len(toks)
    part = B // lax.axis_size("seq")
    return pl.pallas_call(
        functools.partial(prepare_kernel, shards_in),
        out_shape=[
            jax.ShapeDtypeStruct((Q * part, 2 * shards_in * seqs), jnp.bfloat16),
            jax.ShapeDtypeStruct((Q, 1, B), jnp.float32),
        ],
        scratch_shapes=[pltpu.VMEM((Q * part, seqs), jnp.float32)],
        compiler_params=pltpu.CompilerParams(vmem_limit_bytes=VMEM_BYTES),
        cost_estimate=pl.CostEstimate(
            flops=16 * rows * seqs * shards_in, bytes_accessed=4 * rows * seqs * shards_in, transcendentals=0
        ),
        name="prepare",
    )(*map(in_vmem, (*toks, *mine)))


def gradient_kernel(roles, shards_in, opening, cols, count, left, *refs):
    toks, others = refs[:shards_in], refs[shards_in : 2 * shards_in]
    out, tiles, sems = refs[-3:]
    here = lax.axis_index("pos")
    slots = out.shape[0]
    seqs = toks[0].shape[1]
    part = left.shape[0] // Q
    half = part // 2
    lanes = 2 * B
    dims = (((1,), (1,)), ((), ()))
    if opening:
        tiles[...] = jnp.zeros_like(tiles)
        for slot in range(slots):

            @pl.when(slot >= count[0])
            def _(slot=slot):
                copy = pltpu.make_async_copy(tiles, out.at[slot], sems.at[slot, 0])
                copy.start()
                copy.wait()

    block = lax.bitwise_xor(here, jnp.where(jnp.logical_or(here == 0, here == 3), roles[0], roles[1]))
    wanted = [jnp.logical_and(slot < count[0], cols[0, slot] == block) for slot in range(slots)]
    needed = wanted[0]
    for flag in wanted[1:]:
        needed = jnp.logical_or(needed, flag)

    @pl.when(needed)
    def _():
        states = [tok[pl.ds(pl.multiple_of(block * B, B), B), :] for tok in toks]
        lane = lax.broadcasted_iota(jnp.int32, (half, lanes), 1)
        for b in range(0, Q, 4):
            width = min(4, Q - b)
            hots = [
                jnp.concatenate(
                    [jnp.where(ids == b + at, 1.0, 0.0).astype(jnp.bfloat16) for at in range(width)], axis=0
                )
                for ids in states
            ]
            right = jnp.concatenate(hots + [other[b * B : (b + width) * B, :] for other in others], axis=1)
            rows = lax.dot_general(left[...], right, dims, preferred_element_type=jnp.float32)
            if width * B % lanes:
                rows = jnp.concatenate([rows, rows], axis=1)
            for a in range(Q):
                for pair in range(0, width, 2):
                    columns = slice(pair * B, pair * B + lanes)
                    even = rows[a * part : a * part + half, columns]
                    odd = rows[a * part + half : (a + 1) * part, columns]
                    at = (b + pair) * half
                    tiles[a, at : at + half, :] = jnp.where(lane < B, even, pltpu.roll(odd, B, 1))
                    if pair + 1 < width:
                        tiles[a, at + half : at + 2 * half, :] = jnp.where(lane < B, pltpu.roll(even, B, 1), odd)
            for slot in range(slots):

                @pl.when(wanted[slot])
                def _(slot=slot, b=b, width=width):
                    group = pl.ds(b * half, width * half)
                    pltpu.make_async_copy(tiles.at[:, group], out.at[slot, :, group], sems.at[slot, b // 4]).start()

        for b in range(0, Q, 4):
            for slot in range(slots):

                @pl.when(wanted[slot])
                def _(slot=slot, b=b):
                    group = pl.ds(b * half, min(4, Q - b) * half)
                    pltpu.make_async_copy(tiles.at[:, group], out.at[slot, :, group], sems.at[slot, b // 4]).wait()


def gradient(roles, block_cols, block_count, left, toks, others, done):
    slots = block_cols.shape[1]
    rows, seqs = others[0].shape
    shards_in = len(toks)
    part = B // lax.axis_size("seq")
    smem = pl.BlockSpec(memory_space=pltpu.SMEM)
    anywhere, vmem = pl.BlockSpec(memory_space=pl.ANY), pl.BlockSpec(memory_space=pltpu.VMEM)
    operands = [block_cols, block_count, *map(in_vmem, (left, *toks, *others))]
    specs = [smem, smem] + [vmem] * (1 + 2 * shards_in)
    aliases = {}
    if done is not None:
        aliases = {len(operands): 0}
        operands.append(done)
        specs.append(anywhere)
    height = Q * part // 2
    return pl.pallas_call(
        functools.partial(gradient_kernel, roles, shards_in, done is None),
        in_specs=specs,
        out_specs=anywhere,
        out_shape=jax.ShapeDtypeStruct((slots, Q, height, 2 * B), jnp.float32),
        input_output_aliases=aliases,
        scratch_shapes=[
            pltpu.VMEM((Q, height, 2 * B), jnp.float32),
            pltpu.SemaphoreType.DMA((slots, -(-Q // 4))),
        ],
        compiler_params=pltpu.CompilerParams(vmem_limit_bytes=VMEM_BYTES),
        cost_estimate=pl.CostEstimate(
            flops=4 * Q * part * rows * shards_in * seqs,
            bytes_accessed=4 * Q * height * 2 * B + 4 * rows * seqs * shards_in,
            transcendentals=0,
        ),
        name="gradient",
    )(*operands)


def partner(bits, axis):
    return [(i, i ^ bits) for i in range(lax.axis_size(axis))]


def exchanged(value, bits, axis):
    return lax.ppermute(value, axis, partner(bits, axis))


def over_seq(value):
    along = exchanged(value, 2, "seq")
    return [value, along, exchanged(value, 1, "seq"), exchanged(along, 1, "seq")]


def shards_four(couplings, fields, tokens, seq_weights, block_cols, block_count):
    total_seqs = tokens.shape[1] * lax.axis_size("seq")
    steady = lax.optimization_barrier
    near, mid, far = across_terms(couplings, tokens, block_cols, block_count)
    mid, tokens = steady((mid, tokens))
    paired = exchanged(mid, 1, "pos")
    tok_along, tok_core = exchanged(tokens, 2, "seq"), exchanged(tokens, 1, "seq")
    pair = pair_sum(far, paired)
    second = exchanged(near, 1, "pos")
    first = exchanged(pair, 3, "pos")
    toks = [tokens, tok_along, tok_core, exchanged(tok_along, 1, "seq")]
    own = own_terms(couplings, tokens, block_cols, block_count)
    own, toks = steady((own, toks))
    res = residuals(in_vmem(own), in_vmem(first), in_vmem(second), fields, tokens, seq_weights, total_seqs)
    along, near_res, far_res = exchanged(res, 2, "seq"), exchanged(res, 1, "pos"), exchanged(res, 3, "pos")
    near_res, along = steady((near_res, along))
    near_along = exchanged(near_res, 2, "seq")
    left, sums = prepare(toks, [res, along, exchanged(res, 1, "seq"), exchanged(along, 1, "seq")])
    mid_res = exchanged(far_res, 1, "pos")
    far_along = exchanged(far_res, 2, "seq")
    mid_res, near_along, left = steady((mid_res, near_along, left))
    mid_along = exchanged(mid_res, 2, "seq")
    nears = [near_res, near_along, exchanged(near_res, 1, "seq"), exchanged(near_along, 1, "seq")]
    grad = gradient((1, 1), block_cols, block_count, left, toks, nears, None)
    fars = [far_res, far_along, exchanged(far_res, 1, "seq"), exchanged(far_along, 1, "seq")]
    grad = gradient((3, 3), block_cols, block_count, left, toks, fars, grad)
    mid_core = exchanged(mid_res, 1, "seq")
    mid_along, grad, mid_core = steady((mid_along, grad, mid_core))
    mids = [mid_res, mid_along, mid_core, exchanged(mid_along, 1, "seq")]
    grad = gradient((2, 2), block_cols, block_count, left, toks, mids, grad)
    share_len = couplings.shape[-1] // lax.axis_size("seq")
    return (grad.reshape(1, couplings.shape[1], Q, Q, share_len), sums.reshape(1, Q, B))


def solution(mesh):
    placed = (
        P(("grp", "pos"), None, None, None, None),
        P(("grp", "pos"), None, None),
        P("grp", "seq"),
        P(("grp", "seq")),
        P(("grp", "pos"), None),
        P(("grp", "pos")),
    )
    return jax.shard_map(
        shards_four if mesh.shape["pos"] == 4 and mesh.shape["seq"] == 4 else shards,
        mesh=mesh,
        in_specs=placed,
        out_specs=(P(("grp", "pos"), None, None, None, "seq"), P(("grp", "pos"), None, None)),
        check_vma=False,
    )
```

```python
import functools

import jax
import jax.numpy as jnp
from jax import lax
from jax.experimental import pallas as pl
from jax.experimental.pallas import tpu as pltpu
from jax.sharding import PartitionSpec as P

Q = 21
B = 64
VMEM_BYTES = 40 * 1024 * 1024
ACROSS_VMEM_BYTES = 56 * 1024 * 1024
OWN_VMEM_BYTES = 50 * 1024 * 1024


def add_block(total, index, block):
    current = lax.dynamic_index_in_dim(total, index, 0, keepdims=False)
    return lax.dynamic_update_index_in_dim(total, current + block, index, 0)


def gated(is_live, compute):
    values = compute()
    switch = is_live.astype(jnp.float32)
    return tuple((value * switch for value in values))


def pair_matrix(coupling, states, width):
    square = coupling.reshape(states, states, width, width)
    return jnp.transpose(square, (0, 2, 1, 3)).reshape(states * width, states * width)


def pair_rows(res_row, hot_row, res_col, hot_col, row_count, col_count):
    seq_len = res_row.shape[-1]
    dims = (((1,), (1,)), ((), ()))
    first = lax.dot_general(
        res_row.reshape(Q * row_count, seq_len),
        hot_col.reshape(Q * col_count, seq_len),
        dims,
        preferred_element_type=jnp.float32,
    )
    second = lax.dot_general(
        hot_row.reshape(Q * row_count, seq_len),
        res_col.reshape(Q * col_count, seq_len),
        dims,
        preferred_element_type=jnp.float32,
    )
    table = (first + second).reshape(Q, row_count, Q, col_count)
    return jnp.transpose(table, (1, 3, 0, 2)).reshape(row_count * col_count, Q, Q)


def shards(couplings, fields, tokens, seq_weights, block_cols, block_count):
    rows_here, slot_count = block_cols.shape
    positions, seq_here = tokens.shape
    blocks_all = positions // B
    owner_index = lax.axis_index("pos")
    total_seqs = seq_here * lax.axis_size("seq")
    states = jnp.arange(Q, dtype=jnp.int32)
    onehot = (
        tokens.reshape(blocks_all, B, seq_here)[:, None, :, :] == states[None, :, None, None]
    ).astype(jnp.bfloat16)
    block_shape = (Q, B, seq_here)
    partials = jnp.zeros((blocks_all, Q, B, seq_here), jnp.float32)
    local_row = 0
    row_block = owner_index * rows_here + local_row
    hot_row = lax.dynamic_index_in_dim(onehot, row_block, 0, keepdims=False)
    for slot_index in range(slot_count):
        column = block_cols[local_row, slot_index]
        is_live = slot_index < block_count[local_row]
        matrix = pair_matrix(couplings[local_row, slot_index], Q, B)
        hot_col = lax.dynamic_index_in_dim(onehot, column, 0, keepdims=False)

        def contribute(matrix=matrix, hot_col=hot_col, hot_row=hot_row):
            own_term = jnp.dot(
                matrix, hot_col.reshape(Q * B, seq_here), preferred_element_type=jnp.float32
            )
            across = lax.dot_general(
                matrix,
                hot_row.reshape(Q * B, seq_here),
                (((0,), (0,)), ((), ())),
                preferred_element_type=jnp.float32,
            )
            return (own_term.reshape(block_shape), across.reshape(block_shape))

        own_term, across = gated(is_live, contribute)
        partials = add_block(partials, row_block, own_term)
        partials = add_block(partials, column, across)
    summed = lax.psum_scatter(
        partials.astype(jnp.bfloat16), "pos", scatter_dimension=0, tiled=True
    ).astype(jnp.float32)
    logits = summed + fields[..., None]
    softmax_probs = jax.nn.softmax(logits, axis=1)
    own_rows = lax.dynamic_slice_in_dim(onehot, owner_index * rows_here, rows_here, 0).astype(
        jnp.float32
    )
    seq_scale = seq_weights.astype(jnp.float32) / total_seqs
    residual = ((softmax_probs - own_rows) * seq_scale).astype(jnp.bfloat16)
    grad_fields = lax.psum(jnp.sum(residual.astype(jnp.float32), axis=3), "seq")
    residual_all = lax.all_gather(residual, "pos", axis=0, tiled=True)
    share_len = couplings.shape[-1] // lax.axis_size("seq")
    slot_grads = []
    local_row = 0
    row_block = owner_index * rows_here + local_row
    hot_row = lax.dynamic_index_in_dim(onehot, row_block, 0, keepdims=False)
    res_row = lax.dynamic_index_in_dim(residual_all, row_block, 0, keepdims=False)
    for slot_index in range(slot_count):
        column = block_cols[local_row, slot_index]
        is_live = slot_index < block_count[local_row]
        hot_col = lax.dynamic_index_in_dim(onehot, column, 0, keepdims=False)
        res_col = lax.dynamic_index_in_dim(residual_all, column, 0, keepdims=False)

        def slot_term(
            start,
            count,
            hot_row=hot_row,
            res_row=res_row,
            hot_col=hot_col,
            res_col=res_col,
            is_live=is_live,
        ):

            def compute():
                return (pair_rows(res_row, hot_row, res_col, hot_col, count // B, B),)

            (term,) = gated(is_live, compute)
            return term

        share = lax.psum_scatter(
            slot_term(jnp.int32(0), lax.axis_size("seq") * share_len),
            "seq",
            scatter_dimension=0,
            tiled=True,
        )
        slot_grads.append(jnp.transpose(share, (1, 2, 0)))
    grad_couplings = jnp.stack(slot_grads).reshape(rows_here, slot_count, Q, Q, share_len)
    return (grad_couplings, grad_fields)


PIECES = 3


def in_vmem(value):
    return pltpu.with_memory_space_constraint(value, pltpu.VMEM)


def fetch(w, held, arrived, slot, piece):
    states = pl.ds(piece * (Q // PIECES), Q // PIECES)
    return pltpu.make_async_copy(w.at[slot, states], held.at[slot, states], arrived.at[slot, piece])


def fetch_live(w, held, arrived, count):
    for slot in range(w.shape[0]):

        @pl.when(slot < count[0])
        def _(slot=slot):
            for piece in range(PIECES):
                fetch(w, held, arrived, slot, piece).start()


def relay(w, held, arrived, slot, table):
    pairs, lanes = B // 2, 2 * B

    def move(piece, carry):
        fetch(w, held, arrived, slot, piece).wait()
        for sub in range(Q // PIECES):
            a = piece * (Q // PIECES) + sub
            blocks = held[slot, a].reshape(Q, pairs, lanes)
            for b in range(Q):
                table[pl.ds(pl.multiple_of(a * pairs, pairs), pairs), b * lanes : (b + 1) * lanes] = blocks[b]
        return carry

    lax.fori_loop(0, PIECES, move, 0)


def own_kernel(cols, count, w, tok, own, held, arrived, table, hot_col, acc_own):
    slot = pl.program_id(0)
    seqs = tok.shape[1]
    pairs, lanes = B // 2, 2 * B

    @pl.when(slot == 0)
    def _():
        fetch_live(w, held, arrived, count)
        acc_own[...] = jnp.zeros_like(acc_own)
        hot_col[...] = jnp.zeros_like(hot_col)

    @pl.when(slot < count[0])
    def _():
        relay(w, held, arrived, slot, table)
        ids = tok[pl.ds(pl.multiple_of(cols[0, slot] * B, B), B), :]
        for b in range(Q):
            hot = jnp.where(ids == b, 1.0, 0.0).astype(jnp.bfloat16)
            hot_col[b * lanes : b * lanes + B, :seqs] = hot
            hot_col[b * lanes + B : (b + 1) * lanes, seqs:] = hot
        acc_own[...] += jnp.dot(table[...], hot_col[...], preferred_element_type=jnp.float32)

    @pl.when(slot == pl.num_programs(0) - 1)
    def _():
        for odd in range(2):
            own[pl.ds(odd, Q * pairs, stride=2), :] = acc_own[:, odd * seqs : (odd + 1) * seqs]


def across_kernel(cols, count, w, tok, near, mid, far, held, arrived, table, hot_own, acc):
    slot = pl.program_id(0)
    seqs = tok.shape[1]
    pairs = B // 2
    lanes = 2 * B
    here = lax.axis_index("pos")
    lane = lax.broadcasted_iota(jnp.int32, (seqs, lanes), 1)

    @pl.when(slot == 0)
    def _():
        fetch_live(w, held, arrived, count)
        acc[...] = jnp.zeros_like(acc)
        table[Q * pairs :, :] = jnp.zeros((table.shape[0] - Q * pairs, table.shape[1]), table.dtype)
        for odd in range(2):
            ids = tok[pl.ds(here * B + odd, pairs, stride=2), :].astype(jnp.float32)
            ids = jnp.concatenate([ids] * 4, axis=0).T
            for tile in range(table.shape[0] // lanes):
                state = (4 * tile + lane // pairs).astype(jnp.float32)
                hot_own[odd * seqs : (odd + 1) * seqs, tile * lanes : (tile + 1) * lanes] = jnp.where(
                    ids == state, 1.0, 0.0
                ).astype(jnp.bfloat16)

    @pl.when(slot < count[0])
    def _():
        role = lax.bitwise_xor(cols[0, slot], here)
        relay(w, held, arrived, slot, table)
        for b in range(0, Q, 2):
            width = 2 if b + 1 < Q else 1
            part = jnp.dot(
                hot_own[...],
                table[:, b * lanes : (b + width) * lanes],
                preferred_element_type=jnp.float32,
            )
            top0, low0 = part[:seqs, :lanes], part[seqs:, :lanes]
            if width == 2:
                top1, low1 = part[:seqs, lanes:], part[seqs:, lanes:]
            else:
                top1, low1 = top0, low0
            both = jnp.where(lane < B, top0, low1) + pltpu.roll(jnp.where(lane < B, top1, low0), B, 1)
            rows = slice(b * B, (b + width) * B)
            acc[role, rows, :] += both.T[: width * B, :]

    @pl.when(slot == pl.num_programs(0) - 1)
    def _():
        near[...] = acc[1].astype(jnp.bfloat16)
        mid[...] = acc[2].astype(jnp.bfloat16)
        far[...] = acc[3].astype(jnp.bfloat16)


def forward_call(kernel, name, outs, vmem_bytes, scratch, couplings, tokens, block_cols, block_count):
    slots = couplings.shape[1]
    positions, seqs = tokens.shape
    rows = Q * B
    smem = pl.BlockSpec(memory_space=pltpu.SMEM)
    return pl.pallas_call(
        kernel,
        grid=(slots,),
        in_specs=[
            smem,
            smem,
            pl.BlockSpec(memory_space=pl.ANY),
            pl.BlockSpec((positions, seqs), lambda k: (0, 0)),
        ],
        out_specs=[pl.BlockSpec((rows, seqs), lambda k: (0, 0))] * len(outs),
        out_shape=[jax.ShapeDtypeStruct((rows, seqs), dtype) for dtype in outs],
        scratch_shapes=[
            pltpu.VMEM((slots, Q, Q, B * B), couplings.dtype),
            pltpu.SemaphoreType.DMA((slots, PIECES)),
            *scratch,
        ],
        compiler_params=pltpu.CompilerParams(vmem_limit_bytes=vmem_bytes),
        cost_estimate=pl.CostEstimate(
            flops=2 * 4 * slots * rows * rows * seqs, bytes_accessed=2 * couplings.size, transcendentals=0
        ),
        name=name,
    )(block_cols, block_count, couplings.reshape(slots, Q, Q, B * B), tokens)


def across_terms(couplings, tokens, block_cols, block_count):
    seqs, pairs, lanes = tokens.shape[1], B // 2, 2 * B
    depth = -(-Q * pairs // lanes) * lanes
    scratch = [
        pltpu.VMEM((depth, Q * lanes), jnp.bfloat16),
        pltpu.VMEM((2 * seqs, depth), jnp.bfloat16),
        pltpu.VMEM((4, Q * B, seqs), jnp.float32),
    ]
    return forward_call(
        across_kernel, "across", [jnp.bfloat16] * 3, ACROSS_VMEM_BYTES, scratch, couplings, tokens, block_cols, block_count
    )


def own_terms(couplings, tokens, block_cols, block_count):
    seqs, pairs, lanes = tokens.shape[1], B // 2, 2 * B
    scratch = [
        pltpu.VMEM((Q * pairs, Q * lanes), jnp.bfloat16),
        pltpu.VMEM((Q * lanes, 2 * seqs), jnp.bfloat16),
        pltpu.VMEM((Q * pairs, 2 * seqs), jnp.float32),
    ]
    (own,) = forward_call(
        own_kernel, "own", [jnp.float32], OWN_VMEM_BYTES, scratch, couplings, tokens, block_cols, block_count
    )
    return own


def pair_kernel(left, right, out):
    out[...] = (left[...].astype(jnp.float32) + right[...].astype(jnp.float32)).astype(jnp.bfloat16)


def pair_sum(left, right):
    return pl.pallas_call(
        pair_kernel,
        out_shape=jax.ShapeDtypeStruct(left.shape, jnp.bfloat16),
        compiler_params=pltpu.CompilerParams(vmem_limit_bytes=VMEM_BYTES),
        cost_estimate=pl.CostEstimate(flops=left.size, bytes_accessed=6 * left.size, transcendentals=0),
        name="pair_sum",
    )(in_vmem(left), in_vmem(right))


def residual_kernel(total, own, first, second, fields, tok, weights, res):
    here = lax.axis_index("pos")
    step = 16
    scale = weights[...].astype(jnp.float32) / total
    field = fields[0].T
    for start in range(0, B, step):
        ids = tok[pl.ds(pl.multiple_of(here * B + start, step), step), :]
        logits = []
        for a in range(Q):
            rows = slice(a * B + start, a * B + start + step)
            terms = first[rows, :].astype(jnp.float32) + second[rows, :].astype(jnp.float32)
            logits.append(own[rows, :] + terms + field[start : start + step, a : a + 1])
        top = logits[0]
        for a in range(1, Q):
            top = jnp.maximum(top, logits[a])
        powers = [jnp.exp(value - top) for value in logits]
        norm = powers[0]
        for a in range(1, Q):
            norm = norm + powers[a]
        inverse = 1.0 / norm
        for a in range(Q):
            probs = powers[a] * inverse
            res[a * B + start : a * B + start + step, :] = (
                (probs - jnp.where(ids == a, 1.0, 0.0)) * scale
            ).astype(jnp.bfloat16)


def residuals(own, first, second, fields, tokens, seq_weights, total):
    rows, seqs = own.shape
    return pl.pallas_call(
        functools.partial(residual_kernel, total),
        out_shape=jax.ShapeDtypeStruct((rows, seqs), jnp.bfloat16),
        compiler_params=pltpu.CompilerParams(vmem_limit_bytes=VMEM_BYTES),
        cost_estimate=pl.CostEstimate(
            flops=20 * rows * seqs, bytes_accessed=10 * rows * seqs, transcendentals=rows * seqs
        ),
        name="residuals",
    )(own, first, second, fields, tokens, seq_weights.reshape(1, seqs))


def prepare_kernel(shards_in, *refs):
    toks, mine = refs[:shards_in], refs[shards_in : 2 * shards_in]
    left, sums, spread = refs[2 * shards_in :]
    here, share = lax.axis_index("pos"), lax.axis_index("seq")
    seqs = toks[0].shape[1]
    depth = shards_in * seqs
    part = left.shape[0] // Q
    half = part // 2
    ones = jnp.ones((8, seqs), jnp.bfloat16)
    total = sum(
        lax.dot_general(ones, piece[...], (((1,), (1,)), ((), ())), preferred_element_type=jnp.float32)
        for piece in mine
    )
    for a in range(Q):
        sums[a] = total[:1, a * B : (a + 1) * B]
    for n in range(shards_in):
        span = slice(n * seqs, (n + 1) * seqs)
        over = slice(depth + n * seqs, depth + (n + 1) * seqs)
        for a in range(Q):
            start = pl.multiple_of(a * B + share * part, part)
            spread[a * part : (a + 1) * part, :] = mine[n][pl.ds(start, part), :].astype(jnp.float32)
        start = here * B + share * part
        ids = jnp.concatenate([toks[n][pl.ds(start + odd, half, stride=2), :] for odd in range(2)], axis=0)
        for a in range(Q):
            piece = jnp.concatenate(
                [spread[pl.ds(a * part + odd, half, stride=2), :] for odd in range(2)], axis=0
            )
            left[a * part : (a + 1) * part, span] = piece.astype(jnp.bfloat16)
            left[a * part : (a + 1) * part, over] = jnp.where(ids == a, 1.0, 0.0).astype(jnp.bfloat16)


def prepare(toks, mine):
    rows, seqs = mine[0].shape
    shards_in = len(toks)
    part = B // lax.axis_size("seq")
    return pl.pallas_call(
        functools.partial(prepare_kernel, shards_in),
        out_shape=[
            jax.ShapeDtypeStruct((Q * part, 2 * shards_in * seqs), jnp.bfloat16),
            jax.ShapeDtypeStruct((Q, 1, B), jnp.float32),
        ],
        scratch_shapes=[pltpu.VMEM((Q * part, seqs), jnp.float32)],
        compiler_params=pltpu.CompilerParams(vmem_limit_bytes=VMEM_BYTES),
        cost_estimate=pl.CostEstimate(
            flops=16 * rows * seqs * shards_in, bytes_accessed=4 * rows * seqs * shards_in, transcendentals=0
        ),
        name="prepare",
    )(*map(in_vmem, (*toks, *mine)))


def gradient_kernel(roles, shards_in, opening, cols, count, left, *refs):
    toks, others = refs[:shards_in], refs[shards_in : 2 * shards_in]
    out, tiles, sems = refs[-3:]
    here = lax.axis_index("pos")
    slots = out.shape[0]
    seqs = toks[0].shape[1]
    part = left.shape[0] // Q
    half = part // 2
    lanes = 2 * B
    dims = (((1,), (1,)), ((), ()))
    if opening:
        tiles[...] = jnp.zeros_like(tiles)
        for slot in range(slots):

            @pl.when(slot >= count[0])
            def _(slot=slot):
                copy = pltpu.make_async_copy(tiles, out.at[slot], sems.at[slot, 0])
                copy.start()
                copy.wait()

    block = lax.bitwise_xor(here, jnp.where(jnp.logical_or(here == 0, here == 3), roles[0], roles[1]))
    wanted = [jnp.logical_and(slot < count[0], cols[0, slot] == block) for slot in range(slots)]
    needed = wanted[0]
    for flag in wanted[1:]:
        needed = jnp.logical_or(needed, flag)

    @pl.when(needed)
    def _():
        states = [tok[pl.ds(pl.multiple_of(block * B, B), B), :] for tok in toks]
        lane = lax.broadcasted_iota(jnp.int32, (half, lanes), 1)
        for b in range(0, Q, 4):
            width = min(4, Q - b)
            hots = [
                jnp.concatenate(
                    [jnp.where(ids == b + at, 1.0, 0.0).astype(jnp.bfloat16) for at in range(width)], axis=0
                )
                for ids in states
            ]
            right = jnp.concatenate(hots + [other[b * B : (b + width) * B, :] for other in others], axis=1)
            rows = lax.dot_general(left[...], right, dims, preferred_element_type=jnp.float32)
            if width * B % lanes:
                rows = jnp.concatenate([rows, rows], axis=1)
            for a in range(Q):
                for pair in range(0, width, 2):
                    columns = slice(pair * B, pair * B + lanes)
                    even = rows[a * part : a * part + half, columns]
                    odd = rows[a * part + half : (a + 1) * part, columns]
                    at = (b + pair) * half
                    tiles[a, at : at + half, :] = jnp.where(lane < B, even, pltpu.roll(odd, B, 1))
                    if pair + 1 < width:
                        tiles[a, at + half : at + 2 * half, :] = jnp.where(lane < B, pltpu.roll(even, B, 1), odd)
            for slot in range(slots):

                @pl.when(wanted[slot])
                def _(slot=slot, b=b, width=width):
                    group = pl.ds(b * half, width * half)
                    pltpu.make_async_copy(tiles.at[:, group], out.at[slot, :, group], sems.at[slot, b // 4]).start()

        for b in range(0, Q, 4):
            for slot in range(slots):

                @pl.when(wanted[slot])
                def _(slot=slot, b=b):
                    group = pl.ds(b * half, min(4, Q - b) * half)
                    pltpu.make_async_copy(tiles.at[:, group], out.at[slot, :, group], sems.at[slot, b // 4]).wait()


def gradient(roles, block_cols, block_count, left, toks, others, done):
    slots = block_cols.shape[1]
    rows, seqs = others[0].shape
    shards_in = len(toks)
    part = B // lax.axis_size("seq")
    smem = pl.BlockSpec(memory_space=pltpu.SMEM)
    anywhere, vmem = pl.BlockSpec(memory_space=pl.ANY), pl.BlockSpec(memory_space=pltpu.VMEM)
    operands = [block_cols, block_count, *map(in_vmem, (left, *toks, *others))]
    specs = [smem, smem] + [vmem] * (1 + 2 * shards_in)
    aliases = {}
    if done is not None:
        aliases = {len(operands): 0}
        operands.append(done)
        specs.append(anywhere)
    height = Q * part // 2
    return pl.pallas_call(
        functools.partial(gradient_kernel, roles, shards_in, done is None),
        in_specs=specs,
        out_specs=anywhere,
        out_shape=jax.ShapeDtypeStruct((slots, Q, height, 2 * B), jnp.float32),
        input_output_aliases=aliases,
        scratch_shapes=[
            pltpu.VMEM((Q, height, 2 * B), jnp.float32),
            pltpu.SemaphoreType.DMA((slots, -(-Q // 4))),
        ],
        compiler_params=pltpu.CompilerParams(vmem_limit_bytes=VMEM_BYTES),
        cost_estimate=pl.CostEstimate(
            flops=4 * Q * part * rows * shards_in * seqs,
            bytes_accessed=4 * Q * height * 2 * B + 4 * rows * seqs * shards_in,
            transcendentals=0,
        ),
        name="gradient",
    )(*operands)


def partner(bits, axis):
    return [(i, i ^ bits) for i in range(lax.axis_size(axis))]


def exchanged(value, bits, axis):
    return lax.ppermute(value, axis, partner(bits, axis))


def over_seq(value):
    along = exchanged(value, 2, "seq")
    return [value, along, exchanged(value, 1, "seq"), exchanged(along, 1, "seq")]


def shards_four(couplings, fields, tokens, seq_weights, block_cols, block_count):
    total_seqs = tokens.shape[1] * lax.axis_size("seq")
    steady = lax.optimization_barrier
    near, mid, far = across_terms(couplings, tokens, block_cols, block_count)
    paired = exchanged(mid, 1, "pos")
    near, paired, tokens = steady((near, paired, tokens))
    pair = pair_sum(far, paired)
    second = exchanged(near, 1, "pos")
    tok_along, tok_core = exchanged(tokens, 2, "seq"), exchanged(tokens, 1, "seq")
    first = exchanged(pair, 3, "pos")
    toks = [tokens, tok_along, tok_core, exchanged(tok_along, 1, "seq")]
    own = own_terms(couplings, tokens, block_cols, block_count)
    own, toks = steady((own, toks))
    res = residuals(in_vmem(own), in_vmem(first), in_vmem(second), fields, tokens, seq_weights, total_seqs)
    along, near_res, far_res = exchanged(res, 2, "seq"), exchanged(res, 1, "pos"), exchanged(res, 3, "pos")
    near_res, along = steady((near_res, along))
    near_along = exchanged(near_res, 2, "seq")
    left, sums = prepare(toks, [res, along, exchanged(res, 1, "seq"), exchanged(along, 1, "seq")])
    mid_res = exchanged(far_res, 1, "pos")
    far_along = exchanged(far_res, 2, "seq")
    mid_res, near_along, left = steady((mid_res, near_along, left))
    mid_along = exchanged(mid_res, 2, "seq")
    nears = [near_res, near_along, exchanged(near_res, 1, "seq"), exchanged(near_along, 1, "seq")]
    grad = gradient((1, 1), block_cols, block_count, left, toks, nears, None)
    fars = [far_res, far_along, exchanged(far_res, 1, "seq"), exchanged(far_along, 1, "seq")]
    grad = gradient((3, 3), block_cols, block_count, left, toks, fars, grad)
    mid_core = exchanged(mid_res, 1, "seq")
    mid_along, grad, mid_core = steady((mid_along, grad, mid_core))
    mids = [mid_res, mid_along, mid_core, exchanged(mid_along, 1, "seq")]
    grad = gradient((2, 2), block_cols, block_count, left, toks, mids, grad)
    share_len = couplings.shape[-1] // lax.axis_size("seq")
    return (grad.reshape(1, couplings.shape[1], Q, Q, share_len), sums.reshape(1, Q, B))


def solution(mesh):
    placed = (
        P(("grp", "pos"), None, None, None, None),
        P(("grp", "pos"), None, None),
        P("grp", "seq"),
        P(("grp", "seq")),
        P(("grp", "pos"), None),
        P(("grp", "pos")),
    )
    return jax.shard_map(
        shards_four if mesh.shape["pos"] == 4 and mesh.shape["seq"] == 4 else shards,
        mesh=mesh,
        in_specs=placed,
        out_specs=(P(("grp", "pos"), None, None, None, "seq"), P(("grp", "pos"), None, None)),
        check_vma=False,
    )
```
